256 devices in a mesh: dp: 8 (over y, core), space: 32 (over z, x).
Axes of the slice: x: 4, y: 4, z: 8, core: 2. Of those that a mesh axis runs over, the one named last changes fastest.
Arguments:
- features: bfloat16 [8, 96, 32768], P('dp', None, 'space'), may hold values from -6 to 6
- weight_one: bfloat16 [96, 2592], replicated, may hold values from -0.15625 to 0.15625
- weight_down: bfloat16 [256, 768], replicated, may hold values from -0.3125 to 0.3125
- weight_two: bfloat16 [256, 6912], replicated, may hold values from -0.09375 to 0.09375
- cotangent: bfloat16 [8, 256, 8192], P('dp', None, 'space'), may hold values from -6 to 6
- rule_one: int32 [8, 27, 32768], P('dp', None, 'space'), may hold values from -1 to 2047, as said below
- rule_two: int32 [8, 27, 8192], P('dp', None, 'space'), may hold values from -1 to 511, as said below
- children: int32 [8, 8, 8192], P('dp', None, 'space'), may hold values from -1 to 1023, as said below
- send_one: int32 [8, 32, 8, 128], P('dp', 'space'), may hold values from 0 to 1023
- count_one: int32 [8, 32, 8], P('dp', 'space'), may hold values from 0 to 128, as said below
- send_two: int32 [8, 32, 8, 32], P('dp', 'space'), may hold values from 0 to 255
- count_two: int32 [8, 32, 8], P('dp', 'space'), may hold values from 0 to 32, as said below
Outputs:
- coarse_out: bfloat16 [8, 256, 8192], P('dp', None, 'space')
- input_grad: bfloat16 [8, 96, 32768], P('dp', None, 'space')
- grad_w_one: float32 [96, 2592], P('space')
- grad_w_down: float32 [256, 768], P('space')
- grad_w_two: float32 [256, 6912], P('space')
The draws below stay inside these ranges and needn't reach their ends.
Inputs may be any that keep to these rules, and one draw needn't show every extreme that they name: `count_one`: zero where the neighbour in direction d lies outside the grid. `count_two`: zero where the neighbour in direction d lies outside the grid. `rule_one`: each entry is -1, a row below 1024 of the brick itself, or 1024 + d * 128 + j with j below count_one of the sender of slot d; offset 13 maps every voxel to itself. `rule_two`: each entry is -1, a row below 256 of the brick itself, or 256 + d * 32 + j with j below count_two of the sender of slot d; offset 13 maps every voxel to itself. `children`: within a brick's block every fine row appears exactly once; the other entries are -1.
All inputs are finite; a program needn't handle non-finite values.
Results may differ from the reference program's by a relative error of at most 0.025.
Values may be sent and summed in bfloat16 or wider, within the bound.
A program may use at most 128 MiB of HBM per device.

```python
import jax
import jax.numpy as jnp
from jax import lax

C1 = 96
C2 = 256
V = 1024
H1 = 128
H2 = 32
V2 = 256
TILES = 8
N_DP = 8
N_SPACE = 32


directions = ((-1, -1), (-1, 0), (-1, 1), (0, -1), (0, 1), (1, -1), (1, 0), (1, 1))


def grid_tables():
    width_x = N_SPACE // 4
    bricks = jnp.arange(N_SPACE, dtype=jnp.int32)
    step_y = jnp.array([pair[0] for pair in directions], jnp.int32)
    step_x = jnp.array([pair[1] for pair in directions], jnp.int32)
    return (width_x, bricks // width_x, bricks % width_x, step_y, step_x)


def halo_counts(key, capacity):
    width_x, grid_y, grid_x, step_y, step_x = grid_tables()
    near_y = grid_y[:, None] + step_y[None]
    near_x = grid_x[:, None] + step_x[None]
    inside = (near_y >= 0) & (near_y < 4) & (near_x >= 0) & (near_x < width_x)
    facing = step_y * step_x == 0
    larger = jax.random.randint(jax.random.fold_in(key, 1), (TILES, N_SPACE, 8), capacity // 2, capacity + 1)
    smaller = jax.random.randint(jax.random.fold_in(key, 2), (TILES, N_SPACE, 8), 1, max(capacity // 8, 1) + 1)
    counts = jnp.where(facing[None, None], larger, smaller) * inside[None].astype(jnp.int32)
    counts = counts.at[:, 0, 4].set(capacity).at[:, 0, 7].set(capacity)
    return counts.astype(jnp.int32)


def incoming(counts):
    width_x, grid_y, grid_x, step_y, step_x = grid_tables()
    source_y = grid_y[:, None] - step_y[None]
    source_x = grid_x[:, None] - step_x[None]
    inside = (source_y >= 0) & (source_y < 4) & (source_x >= 0) & (source_x < width_x)
    source = jnp.where(inside, source_y * width_x + source_x, 0)
    taken = counts[:, source, jnp.arange(8)[None, :]]
    return taken * inside[None].astype(jnp.int32)


def rule_table(key, counts, capacity, rows):
    received = incoming(counts)
    shape = (TILES, 27, N_SPACE, rows)
    present = jax.random.randint(jax.random.fold_in(key, 3), shape, 0, 20) < 11
    use_halo = jax.random.randint(jax.random.fold_in(key, 4), shape, 0, 4) == 0
    heading = jax.random.randint(jax.random.fold_in(key, 5), shape, 0, 8)
    slot_pick = jax.random.randint(jax.random.fold_in(key, 6), shape, 0, capacity)
    local = jax.random.randint(jax.random.fold_in(key, 7), shape, 0, rows)
    tile_ids = jnp.arange(TILES)[:, None, None, None]
    brick_ids = jnp.arange(N_SPACE)[None, None, :, None]
    have = received[tile_ids, brick_ids, heading]
    halo_pos = rows + heading * capacity + slot_pick % jnp.maximum(have, 1)
    chosen = jnp.where(use_halo & (have > 0), halo_pos, local)
    chosen = jnp.where(present, chosen, -1)
    centre = jnp.arange(27)[None, :, None, None] == 13
    chosen = jnp.where(centre, jnp.arange(rows)[None, None, None, :], chosen)
    chosen = chosen.at[:, 0, N_SPACE // 4 + 1, 0].set(rows + 8 * capacity - 1)
    return chosen.reshape(TILES, 27, N_SPACE * rows).astype(jnp.int32)


def draw_count_one(key, part):
    return halo_counts(jax.random.fold_in(key, 101), H1)


def draw_rule_one(key, part):
    counts = halo_counts(jax.random.fold_in(key, 101), H1)
    key = jax.random.fold_in(key, 11)
    return rule_table(key, counts, H1, V)


def draw_count_two(key, part):
    return halo_counts(jax.random.fold_in(key, 202), H2)


def draw_rule_two(key, part):
    counts = halo_counts(jax.random.fold_in(key, 202), H2)
    key = jax.random.fold_in(key, 12)
    return rule_table(key, counts, H2, V2)


def draw_children(key, part):
    key = jax.random.fold_in(key, 13)
    keys = jax.random.split(key, TILES * N_SPACE)
    orders = jax.vmap(lambda one_key: jax.random.permutation(one_key, 2 * V))(keys)
    chosen = jnp.where(orders < V, orders, -1).reshape(TILES, N_SPACE, 8, V2)
    return chosen.transpose(0, 2, 1, 3).reshape(TILES, 8, N_SPACE * V2).astype(jnp.int32)


def touch_ends(values, own_key, low, high):
    place = [jax.random.randint(jax.random.fold_in(own_key, axis), (), 0, length) for axis, length in enumerate(values.shape)]
    widest = values.shape.index(max(values.shape))
    beside = place[:widest] + [(place[widest] + 1) % values.shape[widest]] + place[widest + 1:]
    return values.at[tuple(place)].set(low).at[tuple(beside)].set(high)


def raised(values, key, source, target, parts, factor):
    def block_of(dim):
        return (jnp.arange(values.shape[dim]) // (values.shape[dim] // parts)).reshape((-1,) + (1,) * (values.ndim - 1 - dim))

    first = jax.random.permutation(key, parts)[block_of(target)]
    far = (block_of(target) + parts // 2) % parts
    return jnp.where((block_of(source) == first) | (block_of(source) == far), factor * values, values)


def steps_of(rng, extent, shards, low, largest):
    def one(dim, parts):
        steps = jax.random.uniform(jax.random.fold_in(jax.random.fold_in(rng, 6), dim), (parts,), jnp.float32, low / len(shards), largest / len(shards))
        return jnp.repeat(jnp.exp(steps), extent[dim] // parts).reshape((-1,) + (1,) * (len(extent) - dim - 1))

    loudness = one(*shards[0])
    for cut in shards[1:]:
        loudness = loudness * one(*cut)
    return loudness


def bell_draw(stream_key, shape, spread, limit, cuts=(), held_as=jnp.bfloat16):
    values = spread * jax.random.normal(stream_key, shape, jnp.float32)
    if cuts:
        values = values * steps_of(stream_key, shape, cuts, -0.22, 0.18)
    return jnp.clip(values, -limit, limit).astype(held_as)


def gaussian_with(own_key, shape, spread, most, shards, heavy, held_as=jnp.bfloat16):
    drawn = spread * jax.random.normal(own_key, shape, jnp.float32)
    if shards:
        drawn = drawn * steps_of(own_key, shape, shards, -0.22, 0.18)
    return jnp.clip(raised(drawn, jax.random.fold_in(own_key, 3), *heavy), -most, most).astype(held_as)


def setup_inputs(seed: int = 0) -> dict:
    key_of = jax.random.split(jax.random.key(seed), 13)
    return {
        "features": bell_draw(key_of[0], (TILES, C1, N_SPACE * V), 1.0, 6.0, ((0, 8), (2, 32))),
        "weight_one": bell_draw(key_of[1], (C1, 27 * C1), (14 * C1) ** -0.5, 0.15625),
        "weight_down": bell_draw(key_of[2], (C2, 8 * C1), (4 * C1) ** -0.5, 0.3125),
        "weight_two": bell_draw(key_of[3], (C2, 27 * C2), (14 * C2) ** -0.5, 0.09375),
        "cotangent": gaussian_with(key_of[4], (TILES, C2, N_SPACE * V2), 1.0, 6.0, ((0, 8), (2, 32)), (2, 1, 32, 2.75)),
        "rule_one": draw_rule_one(jax.random.fold_in(key_of[12], 71), 0),
        "rule_two": draw_rule_two(jax.random.fold_in(key_of[12], 71), 0),
        "children": draw_children(jax.random.fold_in(key_of[12], 71), 0),
        "send_one": touch_ends(jax.random.randint(key_of[8], (TILES, N_SPACE, 8, H1), 0, V), jax.random.fold_in(key_of[8], 1), 0, V - 1).astype(jnp.int32),
        "count_one": draw_count_one(jax.random.fold_in(key_of[12], 71), 0),
        "send_two": touch_ends(jax.random.randint(key_of[10], (TILES, N_SPACE, 8, H2), 0, V2), jax.random.fold_in(key_of[10], 1), 0, V2 - 1).astype(jnp.int32),
        "count_two": draw_count_two(jax.random.fold_in(key_of[12], 71), 0),
    }


directions = ((-1, -1), (-1, 0), (-1, 1), (0, -1), (0, 1), (1, -1), (1, 0), (1, 1))

def silu_grad(value):
    logistic = jax.nn.sigmoid(value)
    return logistic * (1.0 + value * (1.0 - logistic))

def gather_rows(source_table, rule):
    clamped = jnp.maximum(rule, 0)
    picked = jnp.take(source_table, clamped.reshape(-1), axis=1)
    picked = picked.reshape(source_table.shape[0], rule.shape[0], rule.shape[1])
    return picked * (rule >= 0).astype(source_table.dtype)[None]

def conv_apply(weight, picked):
    kernel = weight.reshape(weight.shape[0], picked.shape[1], picked.shape[0]).astype(jnp.float32)
    return jnp.einsum('okc,ckr->or', kernel, picked.astype(jnp.float32))

def weight_term(gradient, picked):
    term = jnp.einsum('or,ckr->okc', gradient.astype(jnp.float32), picked.astype(jnp.float32))
    return term.reshape(gradient.shape[0], -1)

def spread_back(weight, gradient, rule, table_width):
    taps = rule.shape[0]
    kernel = weight.reshape(weight.shape[0], taps, -1).astype(jnp.float32)
    channels = kernel.shape[2]
    grad_float = gradient.astype(jnp.float32)

    def one_tap(offset, running):
        kernel_tap = lax.dynamic_index_in_dim(kernel, offset, 1, keepdims=False)
        row_list = lax.dynamic_index_in_dim(rule, offset, 0, keepdims=False)
        products = jnp.einsum('oc,or->cr', kernel_tap, grad_float)
        products = products * (row_list >= 0).astype(jnp.float32)[None]
        return running.at[:, jnp.maximum(row_list, 0)].add(products)
    return lax.fori_loop(0, taps, one_tap, jnp.zeros((channels, table_width), jnp.float32))

def pack_rows(feature, row_list, row_count):
    picked = jnp.take(feature, row_list.reshape(-1), axis=1)
    picked = picked.reshape(feature.shape[0], row_list.shape[0], row_list.shape[1])
    live_mask = jnp.arange(row_list.shape[1])[None, :] < row_count[:, None]
    return picked * live_mask.astype(feature.dtype)[None]

def unpack_rows(returned, row_list, row_count, table_width):
    live_mask = jnp.arange(row_list.shape[1])[None, :] < row_count[:, None]
    products = (returned * live_mask.astype(jnp.float32)[None]).reshape(returned.shape[0], -1)
    return jnp.zeros((returned.shape[0], table_width), jnp.float32).at[:, row_list.reshape(-1)].add(products)

def receive(packed, sign):
    width_x = N_SPACE // 4
    bricks = jnp.arange(N_SPACE)
    grid_y = bricks // width_x
    grid_x = bricks % width_x
    slots = []
    for position, (step_y, step_x) in enumerate(directions):
        source_y = grid_y - sign * step_y
        source_x = grid_x - sign * step_x
        inside = (source_y >= 0) & (source_y < 4) & (source_x >= 0) & (source_x < width_x)
        source = jnp.where(inside, source_y * width_x + source_x, 0)
        slots.append(packed[source, :, position] * inside.astype(packed.dtype)[:, None, None])
    return jnp.stack(slots, axis=2)

def split_bricks(array, width):
    return array.reshape(array.shape[0], N_SPACE, width).transpose(1, 0, 2)

def join_bricks(array):
    return array.transpose(1, 0, 2).reshape(array.shape[1], -1)

def reference(features, weight_one, weight_down, weight_two, cotangent, rule_one, rule_two, children, send_one, count_one, send_two, count_two):

    def tile_pass(inputs):
        feat_tile, cot_tile, rule_a, rule_b, child_tile, send_a, count_a, send_b, count_b = inputs
        bricks = split_bricks(feat_tile, V)
        upstreams = split_bricks(cot_tile, V2)
        rules_a = split_bricks(rule_a, V)
        rules_b = split_bricks(rule_b, V2)
        child_maps = split_bricks(child_tile, V2)
        halo_one = receive(jax.vmap(pack_rows)(bricks, send_a, count_a), 1)

        def front(item):
            feature, halo, rule, child = item
            ext_one = jnp.concatenate([feature, halo.reshape(feature.shape[0], -1)], axis=1)
            act_one = conv_apply(weight_one, gather_rows(ext_one, rule))
            level_one = (feature.astype(jnp.float32) + jax.nn.silu(act_one)).astype(jnp.bfloat16)
            act_down = conv_apply(weight_down, gather_rows(level_one, child))
            coarse = jax.nn.silu(act_down).astype(jnp.bfloat16)
            return (act_one, level_one, act_down, coarse)
        act_one, level_one, act_down, coarse = lax.map(front, (bricks, halo_one, rules_a, child_maps))
        halo_two = receive(jax.vmap(pack_rows)(coarse, send_b, count_b), 1)

        def back_two(item):
            coarse_brick, halo, rule, upstream = item
            ext_two = jnp.concatenate([coarse_brick, halo.reshape(coarse_brick.shape[0], -1)], axis=1)
            picked_two = gather_rows(ext_two, rule)
            act_two = conv_apply(weight_two, picked_two)
            result = (coarse_brick.astype(jnp.float32) + jax.nn.silu(act_two)).astype(jnp.bfloat16)
            grad_two = (upstream.astype(jnp.float32) * silu_grad(act_two)).astype(jnp.bfloat16)
            return (result, weight_term(grad_two, picked_two), spread_back(weight_two, grad_two, rule, V2 + 8 * H2))
        coarse_out, term_two, ext_grad_two = lax.map(back_two, (coarse, halo_two, rules_b, upstreams))
        returned_two = receive(ext_grad_two[:, :, V2:].reshape(N_SPACE, C2, 8, H2), -1)

        def back_one(item):
            feature, halo, rule, child, level, act_a, act_b, upstream, ext_grad, returned, row_list, row_count = item
            grad_coarse = upstream.astype(jnp.float32) + ext_grad[:, :V2] + unpack_rows(returned, row_list, row_count, V2)
            grad_down = (grad_coarse * silu_grad(act_b)).astype(jnp.bfloat16)
            term_down = weight_term(grad_down, gather_rows(level, child))
            grad_level = spread_back(weight_down, grad_down, child, V)
            grad_one = (grad_level * silu_grad(act_a)).astype(jnp.bfloat16)
            ext_one = jnp.concatenate([feature, halo.reshape(feature.shape[0], -1)], axis=1)
            term_one = weight_term(grad_one, gather_rows(ext_one, rule))
            ext_grad_one = spread_back(weight_one, grad_one, rule, V + 8 * H1)
            return (grad_level, term_down, term_one, ext_grad_one)
        grad_level, term_down, term_one, ext_grad_one = lax.map(back_one, (bricks, halo_one, rules_a, child_maps, level_one, act_one, act_down, upstreams, ext_grad_two, returned_two, send_b, count_b))
        returned_one = receive(ext_grad_one[:, :, V:].reshape(N_SPACE, C1, 8, H1), -1)
        spread_rows = jax.vmap(lambda returned, row_list, row_count: unpack_rows(returned, row_list, row_count, V))
        input_grad = (grad_level + ext_grad_one[:, :, :V] + spread_rows(returned_one, send_a, count_a)).astype(jnp.bfloat16)
        return (join_bricks(coarse_out), join_bricks(input_grad), term_one.sum(0), term_down.sum(0), term_two.sum(0))
    results = lax.map(tile_pass, (features, cotangent, rule_one, rule_two, children, send_one, count_one, send_two, count_two))
    scale = 1.0 / (N_DP * N_SPACE)
    return (results[0], results[1], results[2].sum(0) * scale, results[3].sum(0) * scale, results[4].sum(0) * scale)
```

```python
import jax
import jax.numpy as jnp
from jax import lax
from jax.experimental import pallas as pl
from jax.experimental.pallas import tpu as pltpu
from jax.sharding import PartitionSpec as P

bf16 = jnp.bfloat16
f32 = jnp.float32
i32 = jnp.int32
C1, C2, V, V2, H1, H2, TAPS = 96, 256, 1024, 256, 128, 32, 27
WIDE = 896
THIN = 256
directions = ((-1, -1), (-1, 0), (-1, 1), (0, -1), (0, 1), (1, -1), (1, 0), (1, 1))
ring_place = (0, 2, 3, 1)


def dot(a, b):
    return jnp.dot(a, b, preferred_element_type=f32)


def dot_nt(a, b):
    return lax.dot_general(a, b, (((1,), (1,)), ((), ())), preferred_element_type=f32)


def dot_tn(a, b):
    return lax.dot_general(a, b, (((0,), (0,)), ((), ())), preferred_element_type=f32)


def one_hot(row, size):
    return jnp.where(
        lax.broadcasted_iota(jnp.int16, (size, row.shape[1]), 0) == row.astype(jnp.int16),
        jnp.ones((), bf16),
        jnp.zeros((), bf16),
    )


def logistic(v):
    return 1.0 / (1.0 + jnp.exp(-v))


def silu(v):
    return v * logistic(v)


def silu_grad(v):
    s = logistic(v)
    return s * (1.0 + v * (1.0 - s))


def place():
    return lax.axis_index("dp"), lax.axis_index("space")


def remote(src, dst, send_sem, recv_sem, device):
    return pltpu.make_async_remote_copy(
        src_ref=src,
        dst_ref=dst,
        send_sem=send_sem,
        recv_sem=recv_sem,
        device_id=device,
        device_id_type=pl.DeviceIdType.MESH,
    )


def greet(devices):
    barrier = pltpu.get_barrier_semaphore()
    for device in devices:
        pl.semaphore_signal(barrier, inc=1, device_id=device, device_id_type=pl.DeviceIdType.MESH)
    pl.semaphore_wait(barrier, len(devices))


class Position:
    def __init__(self):
        self.dp, self.space = place()
        self.y, self.core = self.dp // 2, self.dp % 2
        self.z, self.x = self.space // 4, self.space % 4
        self.far, self.near = self.z // 2, self.z % 2

    def brick(self, direction, sign):
        dy, dx = directions[direction]
        gy = (self.space // 8 + sign * dy + 4) % 4
        gx = (self.space % 8 + sign * dx + 8) % 8
        return (self.dp, gy * 8 + gx)

    def other_core(self):
        return (self.y * 2 + 1 - self.core, self.space)

    def at_y(self, y):
        return (y * 2 + self.core, self.space)

    def at_x(self, x):
        return (self.dp, self.z * 4 + x)

    def at_z(self, z):
        return (self.dp, z * 4 + self.x)

    def gray(self, v):
        return (v + v // 2) % 2

    def flip(self, v):
        return v + 1 - 2 * (v % 2)

    def halving(self, axis, step):
        if axis == "z":
            return self.near, self.at_z(self.flip(self.z))
        v, at = (self.y, self.at_y) if axis == "y" else (self.x, self.at_x)
        if step == 0:
            return self.gray(v), at(self.flip(v))
        return v // 2, at(3 - v)

    def targets(self):
        y = (self.far + 1) % 4
        space = (self.y * 2 + self.near) * 4 + self.x
        return [(y * 2 + c, space) for c in range(2)]

    def sources(self):
        far = (self.y + 3) % 4
        return [(self.far * 2 + c, (far * 2 + self.near) * 4 + self.x) for c in range(2)]

    def partners(self):
        return (
            [self.brick(d, 1) for d in range(8)]
            + [self.other_core()]
            + [self.halving(axis, step)[1] for axis in "yx" for step in range(2)]
            + [self.halving("z", 0)[1]]
            + [self.at_z((self.z + 2 * j) % 8) for j in range(1, 4)]
            + self.sources()
        )


def add_into(target, index, source, start, count):
    chunk = min(count, 4)

    def part(i, _):
        here = index + (pl.ds(start + i * chunk, chunk),)
        total = target[here].astype(f32) + source[pl.ds(i * chunk, chunk)].astype(f32)
        target[here] = total.astype(bf16)
        return 0

    lax.fori_loop(0, count // chunk, part, 0)


class Reduction:
    orders = (
        (("y", 0), ("y", 1), ("x", 0), ("x", 1), ("z", 0)),
        (("x", 0), ("x", 1), ("y", 0), ("y", 1), ("z", 0)),
    )

    def __init__(self, pos, buf, from_core, from_step, from_far, summed, landed, send, recv):
        self.pos, self.buf, self.from_core, self.from_step = pos, buf, from_core, from_step
        self.from_far, self.summed, self.landed = from_far, summed, landed
        self.send, self.recv = send, recv

    def core_copy(self):
        return remote(
            self.buf.at[1 - self.pos.core],
            self.from_core,
            self.send.at[0],
            self.recv.at[0],
            self.pos.other_core(),
        )

    def base(self, half, steps):
        start, size = 0, 32
        for axis, step in self.orders[half][:steps]:
            size //= 2
            start = start + self.pos.halving(axis, step)[0] * size
        return start

    def step_copy(self, half, number):
        size = 16 >> number
        keep, partner = self.pos.halving(*self.orders[half][number])
        start = self.base(half, number) + (1 - keep) * size
        sem = 1 + half * 5 + number
        return remote(
            self.buf.at[self.pos.core, half, pl.ds(start, size)],
            self.from_step.at[half, pl.ds(32 - 2 * size, size)],
            self.send.at[sem],
            self.recv.at[sem],
            partner,
        )

    def far_copy(self, j):
        pos = self.pos
        return remote(
            self.from_far.at[pos.far],
            self.from_far.at[pos.far],
            self.send.at[10 + j],
            self.recv.at[11 + pos.far],
            pos.at_z((pos.z + 2 * j) % 8),
        )

    def far_arrival(self, j):
        pos = self.pos
        slot = (pos.far + j) % 4
        return remote(
            self.from_far.at[slot],
            self.from_far.at[slot],
            self.send.at[10 + j],
            self.recv.at[11 + slot],
            pos.at_z((pos.z + 2 * j) % 8),
        )

    def delivery(self, t):
        return remote(
            self.summed,
            self.landed.at[self.pos.core],
            self.send.at[14 + t],
            self.recv.at[15 + self.pos.core],
            self.pos.targets()[t],
        )

    def arrival(self, c):
        return remote(
            self.summed,
            self.landed.at[c],
            self.send.at[14],
            self.recv.at[15 + c],
            self.pos.sources()[c],
        )

    def stage(self, number):
        pos = self.pos
        if number == 1:
            self.core_copy().wait()
            for half in range(2):
                add_into(self.buf, (pos.core, half), self.from_core.at[half], 0, 32)
        if 2 <= number <= 6:
            for half in range(2):
                self.step_copy(half, number - 2).wait()
                size = 16 >> (number - 2)
                add_into(
                    self.buf,
                    (pos.core, half),
                    self.from_step.at[half, pl.ds(32 - 2 * size, size)],
                    self.base(half, number - 1),
                    size,
                )
        if number == 0:
            self.core_copy().start()
        elif number <= 5:
            for half in range(2):
                self.step_copy(half, number - 1).start()
        elif number == 6:
            for half in range(2):
                self.from_far[pos.far, half] = self.buf[pos.core, half, self.base(half, 5)]
            for j in range(1, 4):
                self.far_copy(j).start()
        elif number == 7:
            for j in range(1, 4):
                self.far_copy(j).wait_send()
                self.far_arrival(j).wait_recv()
            total = self.from_far[0].astype(f32)
            for slot in range(1, 4):
                total = total + self.from_far[slot].astype(f32)
            self.summed[...] = total.astype(bf16)
            for t in range(2):
                self.delivery(t).start()
        elif number == 8:
            for t in range(2):
                self.delivery(t).wait_send()
            for c in range(2):
                self.arrival(c).wait_recv()


def block_index(half, space):
    z, x = space // 4, space % 4
    q, p = ring_place[z // 2], ring_place[x]
    return (q * 8 + p * 2 + z % 2) if half == 0 else (p * 8 + q * 2 + z % 2)


def kernel(
    feature,
    w1,
    wd,
    w2,
    upstream,
    rule1,
    rule2,
    child,
    send1,
    send2,
    count1,
    count2,
    coarse_out,
    input_grad,
    gw1,
    gwd,
    gw2,
    ext1,
    pack1,
    picked1,
    act1,
    level,
    pickedd,
    actd,
    coarse,
    pack2,
    halo2,
    ext2,
    picked2,
    back2,
    ext_grad2,
    give2,
    take2,
    grad_level,
    back1,
    ext_grad1,
    give1,
    take1,
    strips,
    wide_buf,
    wide_core,
    wide_step,
    wide_far,
    wide_sum,
    wide_land,
    thin_buf,
    thin_core,
    thin_step,
    thin_far,
    thin_sum,
    thin_land,
    halo_send,
    halo_recv,
    wide_send,
    wide_recv,
    thin_send,
    thin_recv,
):
    pos = Position()
    wide = Reduction(
        pos, wide_buf, wide_core, wide_step, wide_far, wide_sum, wide_land, wide_send, wide_recv
    )
    thin = Reduction(
        pos, thin_buf, thin_core, thin_step, thin_far, thin_sum, thin_land, thin_send, thin_recv
    )

    def live_rows(rows, counts, width):
        lane = lax.broadcasted_iota(i32, (1, width), 1)
        return jnp.concatenate(
            [jnp.where(lane < counts[d], rows[d : d + 1, :], -1) for d in range(8)], axis=1
        )

    def exchange(number, source, target, sign):
        return [
            remote(
                source(d),
                target(d),
                halo_send.at[number, d],
                halo_recv.at[number, d],
                pos.brick(d, sign),
            )
            for d in range(8)
        ]

    live1 = live_rows(send1, count1, H1)
    packed = dot(feature[...], one_hot(live1, V)).astype(bf16)
    for d in range(8):
        pack1[d] = packed[:, d * H1 : (d + 1) * H1]
    ext1[:C1, :] = feature[...]
    greet(pos.partners())
    copies = exchange(
        0, lambda d: pack1.at[d], lambda d: ext1.at[pl.ds(C1, C1), pl.ds(d * H1, H1)], 1
    )
    for copy in copies:
        copy.start()
    strips[...] = jnp.zeros_like(strips)
    picked2[TAPS * C2 :, :] = jnp.zeros((128, C2), bf16)
    for copy in copies:
        copy.wait()

    def tap_one(k, _):
        row = rule1[pl.ds(k, 1), :]
        both = dot(ext1[...], one_hot(jnp.where(row < 0, -1, row & (V - 1)), V))
        mine = jnp.where(row >= V, both[C1:], both[:C1]).astype(bf16)
        picked1[pl.ds(pl.multiple_of(k * C1, C1), C1), :] = mine
        return 0

    lax.fori_loop(0, TAPS, tap_one, 0)
    act = dot(w1[...], picked1[...])
    act1[...] = act
    level[...] = (feature[...].astype(f32) + silu(act)).astype(bf16)

    def tap_down(m, _):
        mine = dot(level[...], one_hot(child[pl.ds(m, 1), :], V)).astype(bf16)
        pickedd[pl.ds(pl.multiple_of(m * C1, C1), C1), :] = mine
        return 0

    lax.fori_loop(0, 8, tap_down, 0)
    act = dot(wd[...], pickedd[...])
    actd[...] = act
    coarse[...] = silu(act).astype(bf16)

    live2 = live_rows(send2, count2, H2)
    pack2[...] = dot(coarse[...], one_hot(live2, V2)).T.astype(bf16)
    copies = exchange(
        1, lambda d: pack2.at[pl.ds(d * H2, H2)], lambda d: halo2.at[pl.ds(d * H2, H2)], 1
    )
    for copy in copies:
        copy.start()
    ext2[:, :V2] = coarse[...]
    for copy in copies:
        copy.wait()
    ext2[:, V2:] = halo2[...].astype(f32).T.astype(bf16)

    def tap_two(k, _):
        mine = dot(ext2[...], one_hot(rule2[pl.ds(k, 1), :], 2 * V2)).astype(bf16)
        picked2[pl.ds(pl.multiple_of(k * C2, C2), C2), :] = mine
        return 0

    lax.fori_loop(0, TAPS, tap_two, 0)
    act = dot(w2[...], picked2[: TAPS * C2, :])
    coarse_out[...] = (coarse[...].astype(f32) + silu(act)).astype(bf16)
    grad_two = (upstream[...].astype(f32) * silu_grad(act)).astype(bf16)

    def spread_two(first):
        ext_grad2[...] = jnp.zeros_like(ext_grad2)

        def taps(t, _):
            rows, hots = [], []
            for k in range(3):
                row = rule2[pl.ds(t * 3 + k, 1), :]
                hots.append(one_hot(jnp.where(row < 0, -1, row - first), V2))
                rows.append(back2[pl.ds(pl.multiple_of((t * 3 + k) * C2, C2), C2), :])
            ext_grad2[...] += dot_nt(
                jnp.concatenate(rows, axis=1), jnp.concatenate(hots, axis=1)
            )
            return 0

        lax.fori_loop(0, TAPS // 3, taps, 0)

    back2[...] = dot_tn(w2[...], grad_two).astype(bf16)
    spread_two(V2)
    give2[...] = ext_grad2[...].T.astype(bf16)
    copies = exchange(
        2, lambda d: give2.at[pl.ds(d * H2, H2)], lambda d: take2.at[pl.ds(d * H2, H2)], -1
    )
    for copy in copies:
        copy.start()
    for quarter in range(4):
        upper = dot_nt(grad_two, picked2[quarter * WIDE : (quarter + 1) * WIDE, :])
        start = TAPS * V2 // 2 + quarter * WIDE
        lower = dot_nt(grad_two, picked2[start : start + WIDE, :])
        both = jnp.concatenate([upper.reshape(32, 8, WIDE), lower.reshape(32, 8, WIDE)], axis=1)
        both = both.astype(bf16)
        for space in range(32):
            wide_buf[quarter // 2, quarter % 2, block_index(quarter % 2, space)] = both[space]
    wide.stage(0)
    spread_two(0)
    for copy in copies:
        copy.wait()
    returned = dot(one_hot(live2, V2), take2[...]).T
    grad_coarse = upstream[...].astype(f32) + ext_grad2[...] + returned
    grad_down = (grad_coarse * silu_grad(actd[...])).astype(bf16)

    back1[: 8 * C1, :V2] = dot_tn(wd[...], grad_down).astype(bf16)
    grad_level[...] = jnp.zeros_like(grad_level)

    def untap_down(m, _):
        mine = back1[pl.ds(pl.multiple_of(m * C1, C1), C1), :V2]
        grad_level[...] += dot_nt(mine, one_hot(child[pl.ds(m, 1), :], V))
        return 0

    lax.fori_loop(0, 8, untap_down, 0)
    wide.stage(1)
    grad_one = (grad_level[...] * silu_grad(act1[...])).astype(bf16)
    term_down = dot_nt(grad_down, pickedd[...]).reshape(32, 8, 768)
    term_one = dot_nt(grad_one, picked1[...]).astype(bf16)
    for q in range(5):
        width = min(640, TAPS * C1 - q * 640)
        strips[q * C1 : (q + 1) * C1, :width] = term_one[:, q * 640 : q * 640 + width]
    spot = lax.broadcasted_iota(i32, (1, 5 * C1), 1)
    strip, out_row = spot // C1, spot % C1
    spot = (out_row // 3) * 16 + (out_row % 3) * 5 + strip
    first = dot(one_hot(spot, 512), strips[...]).reshape(32, 16, 640)
    other = jnp.concatenate([term_down[:, :, :384], term_down[:, :, 384:]], axis=1)
    for quarter in range(4):
        low, high = quarter * THIN, (quarter + 1) * THIN
        if high <= 640:
            both = first[:, :, low:high]
        elif low >= 640:
            both = other[:, :, low - 640 : high - 640]
        else:
            both = jnp.concatenate([first[:, :, low:], other[:, :, : high - 640]], axis=2)
        both = both.astype(bf16)
        for space in range(32):
            thin_buf[quarter // 2, quarter % 2, block_index(quarter % 2, space)] = both[space]
    thin.stage(0)

    back1[...] = dot_tn(w1[...], grad_one).astype(bf16)
    ext_grad1[...] = jnp.zeros_like(ext_grad1)
    beside = {3: (2, 1), 8: (3, 2), 12: (4, 3), 15: (5, 4), 18: (6, 5), 21: (7, 6), 24: (8, 7)}

    def untap_one(k, _):
        for when, (wide_stage, thin_stage) in beside.items():

            @pl.when(k == when)
            def _():
                wide.stage(wide_stage)
                thin.stage(thin_stage)

        row = rule1[pl.ds(k, 1), :]
        mine = back1[pl.ds(pl.multiple_of(k * C1, C1), C1), :]
        zero = jnp.zeros_like(mine)
        both = jnp.concatenate(
            [jnp.where(row >= V, zero, mine), jnp.where(row >= V, mine, zero)], axis=0
        )
        ext_grad1[...] += dot_nt(both, one_hot(jnp.where(row < 0, -1, row & (V - 1)), V))
        return 0

    lax.fori_loop(0, TAPS, untap_one, 0)
    for d in range(8):
        give1[d] = ext_grad1[C1:, d * H1 : (d + 1) * H1].astype(bf16)
    copies = exchange(
        3, lambda d: give1.at[d], lambda d: take1.at[:, pl.ds(d * H1, H1)], -1
    )
    for copy in copies:
        copy.start()
    thin.stage(8)
    scale = 1.0 / 256
    for quarter in range(4):
        piece = wide_land[quarter // 2, quarter % 2].astype(f32) * scale
        for side in range(2):
            start = quarter * WIDE
            width = min(WIDE, TAPS * V2 // 2 - start)
            gw2[:, pl.ds(side * TAPS * V2 // 2 + start, width)] = piece[side * 8 : side * 8 + 8, :width]
    thin_all = jnp.concatenate([thin_land[q // 2, q % 2].astype(f32) for q in range(4)], axis=1) * scale
    gwd[:, :384] = thin_all[:8, 640:]
    gwd[:, 384:] = thin_all[8:, 640:]
    for r in range(3):
        for q in range(5):
            width = min(640, TAPS * C1 - q * 640)
            gw1[r : r + 1, q * 640 : q * 640 + width] = thin_all[r * 5 + q : r * 5 + q + 1, :width]
    for copy in copies:
        copy.wait()
    returned = dot_nt(take1[...], one_hot(live1, V))
    input_grad[...] = (grad_level[...] + ext_grad1[:C1, :] + returned).astype(bf16)


def reduction_scratch(lanes):
    return [
        pltpu.VMEM((2, 2, 32, 16, lanes), bf16),
        pltpu.VMEM((2, 32, 16, lanes), bf16),
        pltpu.VMEM((2, 32, 16, lanes), bf16),
        pltpu.VMEM((4, 2, 16, lanes), bf16),
        pltpu.VMEM((2, 16, lanes), bf16),
        pltpu.VMEM((2, 2, 16, lanes), bf16),
    ]


def run_kernel(*operands):
    vmem = pl.BlockSpec(memory_space=pltpu.VMEM)
    smem = pl.BlockSpec(memory_space=pltpu.SMEM)
    dma = pltpu.SemaphoreType.DMA
    return pl.pallas_call(
        kernel,
        out_shape=(
            jax.ShapeDtypeStruct((C2, V2), bf16),
            jax.ShapeDtypeStruct((C1, V), bf16),
            jax.ShapeDtypeStruct((3, TAPS * C1), f32),
            jax.ShapeDtypeStruct((8, 8 * C1), f32),
            jax.ShapeDtypeStruct((8, TAPS * C2), f32),
        ),
        in_specs=[vmem] * 10 + [smem] * 2,
        out_specs=[vmem] * 5,
        scratch_shapes=[
            pltpu.VMEM((2 * C1, V), bf16),
            pltpu.VMEM((8, C1, H1), bf16),
            pltpu.VMEM((TAPS * C1, V), bf16),
            pltpu.VMEM((C1, V), f32),
            pltpu.VMEM((C1, V), bf16),
            pltpu.VMEM((8 * C1, V2), bf16),
            pltpu.VMEM((C2, V2), f32),
            pltpu.VMEM((C2, V2), bf16),
            pltpu.VMEM((V2, C2), bf16),
            pltpu.VMEM((V2, C2), bf16),
            pltpu.VMEM((C2, 2 * V2), bf16),
            pltpu.VMEM((TAPS * C2 + 128, V2), bf16),
            pltpu.VMEM((TAPS * C2, V2), bf16),
            pltpu.VMEM((C2, V2), f32),
            pltpu.VMEM((V2, C2), bf16),
            pltpu.VMEM((V2, C2), bf16),
            pltpu.VMEM((C1, V), f32),
            pltpu.VMEM((TAPS * C1, V), bf16),
            pltpu.VMEM((2 * C1, V), f32),
            pltpu.VMEM((8, C1, H1), bf16),
            pltpu.VMEM((C1, V), bf16),
            pltpu.VMEM((5 * C1, 640), bf16),
            *reduction_scratch(WIDE),
            *reduction_scratch(THIN),
            dma((4, 8)),
            dma((4, 8)),
            dma((16,)),
            dma((17,)),
            dma((16,)),
            dma((17,)),
        ],
        compiler_params=pltpu.CompilerParams(
            collective_id=0, has_side_effects=True, vmem_limit_bytes=58 << 20
        ),
    )(*operands)


def body(
    features,
    weight_one,
    weight_down,
    weight_two,
    cotangent,
    rule_one,
    rule_two,
    children,
    send_one,
    count_one,
    send_two,
    count_two,
):
    coarse_out, input_grad, gw1, gwd, gw2 = run_kernel(
        features[0],
        weight_one,
        weight_down,
        weight_two,
        cotangent[0],
        rule_one[0],
        rule_two[0],
        children[0],
        send_one[0, 0],
        send_two[0, 0],
        count_one[0, 0],
        count_two[0, 0],
    )
    return coarse_out[None], input_grad[None], gw1, gwd, gw2


def solution(mesh):
    tile = P("dp", None, "space")
    brick = P("dp", "space", None, None)
    count = P("dp", "space", None)
    return jax.shard_map(
        body,
        mesh=mesh,
        in_specs=(tile, P(), P(), P(), tile, tile, tile, tile, brick, count, brick, count),
        out_specs=(tile, tile, P("space", None), P("space", None), P("space", None)),
        check_vma=False,
    )
```

```python
import jax
import jax.numpy as jnp
from jax import lax
from jax.experimental import pallas as pl
from jax.experimental.pallas import tpu as pltpu
from jax.sharding import PartitionSpec as P

bf16 = jnp.bfloat16
f32 = jnp.float32
i32 = jnp.int32
C1, C2, V, V2, H1, H2, TAPS = 96, 256, 1024, 256, 128, 32, 27
WIDE = 896
THIN = 256
directions = ((-1, -1), (-1, 0), (-1, 1), (0, -1), (0, 1), (1, -1), (1, 0), (1, 1))
ring_place = ((0, 2, 3, 1), (0, 1, 3, 2))


def dot(a, b):
    return jnp.dot(a, b, preferred_element_type=f32)


def dot_nt(a, b):
    return lax.dot_general(a, b, (((1,), (1,)), ((), ())), preferred_element_type=f32)


def dot_tn(a, b):
    return lax.dot_general(a, b, (((0,), (0,)), ((), ())), preferred_element_type=f32)


def one_hot(row, size):
    return jnp.where(
        lax.broadcasted_iota(jnp.int16, (size, row.shape[1]), 0) == row.astype(jnp.int16),
        jnp.ones((), bf16),
        jnp.zeros((), bf16),
    )


def logistic(v):
    return 1.0 / (1.0 + jnp.exp(-v))


def silu(v):
    return v * logistic(v)


def silu_grad(v):
    s = logistic(v)
    return s * (1.0 + v * (1.0 - s))


def place():
    return lax.axis_index("dp"), lax.axis_index("space")


def remote(src, dst, send_sem, recv_sem, device):
    return pltpu.make_async_remote_copy(
        src_ref=src,
        dst_ref=dst,
        send_sem=send_sem,
        recv_sem=recv_sem,
        device_id=device,
        device_id_type=pl.DeviceIdType.MESH,
    )


def greet(devices):
    barrier = pltpu.get_barrier_semaphore()
    for device in devices:
        pl.semaphore_signal(barrier, inc=1, device_id=device, device_id_type=pl.DeviceIdType.MESH)


def await_greetings(devices):
    pl.semaphore_wait(pltpu.get_barrier_semaphore(), len(devices))


def in_table(row, first):
    return jnp.where((row >= first) & (row < first + V), row & 255, -1)


def gather_four(table, row, first):
    both = dot(table, one_hot(in_table(row, first), 256))
    odd, upper = (row & 256) != 0, (row & 512) != 0
    low = jnp.where(odd, both[C1 : 2 * C1], both[:C1])
    high = jnp.where(odd, both[3 * C1 :], both[2 * C1 : 3 * C1])
    return jnp.where(upper, high, low).astype(bf16)


def scatter_four(values, row, first):
    place_four = (row >> 8) & 3
    zero = jnp.zeros_like(values)
    spread = jnp.concatenate(
        [jnp.where(place_four == w, values, zero) for w in range(4)], axis=0
    )
    return dot_nt(spread, one_hot(in_table(row, first), 256))


class Position:
    def __init__(self):
        self.dp, self.space = place()
        self.y, self.core = self.dp // 2, self.dp % 2
        self.z, self.x = self.space // 4, self.space % 4
        self.far, self.near = self.z // 2, self.z % 2
        self.half = self.gray(self.far)

    def brick(self, direction, sign):
        dy, dx = directions[direction]
        gy = (self.space // 8 + sign * dy + 4) % 4
        gx = (self.space % 8 + sign * dx + 8) % 8
        return (self.dp, gy * 8 + gx)

    def other_core(self):
        return (self.y * 2 + 1 - self.core, self.space)

    def at_y(self, y):
        return (y * 2 + self.core, self.space)

    def at_x(self, x):
        return (self.dp, self.z * 4 + x)

    def at_z(self, z):
        return (self.dp, z * 4 + self.x)

    def at_far(self, far):
        return self.at_z(far * 2 + self.near)

    def gray(self, v):
        return (v + v // 2) % 2

    def flip(self, v):
        return v + 1 - 2 * (v % 2)

    def halving(self, axis, step):
        if axis == "z":
            return self.near, self.at_z(self.flip(self.z))
        v, at = (self.y, self.at_y) if axis == "y" else (self.x, self.at_x)
        first = 1 - self.core if step == 0 else self.core
        keep = first * self.gray(v) + (1 - first) * (v // 2)
        return keep, at(first * self.flip(v) + (1 - first) * (3 - v))

    def targets(self):
        space = (self.y * 2 + self.near) * 4 + self.x
        y = 2 * (1 - self.far // 2)
        return [((y + i) * 2 + c, space) for i in range(2) for c in range(2)]

    def sources(self):
        pair = 1 - self.y // 2
        spaces = [(2 * (2 * pair + h + pair - 2 * h * pair) + self.near) * 4 + self.x for h in range(2)]
        return [[(self.far * 2 + c, spaces[h]) for h in range(2)] for c in range(2)]

    def partners(self):
        return (
            [self.brick(d, 1) for d in range(8)]
            + [self.other_core()]
            + [self.halving(axis, step)[1] for axis in "yx" for step in range(2)]
            + [self.halving("z", 0)[1], self.at_far(self.flip(self.far)), self.at_far(3 - self.far)]
            + [source for pair in self.sources() for source in pair]
        )


def add_into(target, index, source, start, count):
    chunk = min(count, 4)

    def part(i, _):
        here = index + (pl.ds(start + i * chunk, chunk),)
        total = target[here].astype(f32) + source[pl.ds(i * chunk, chunk)].astype(f32)
        target[here] = total.astype(bf16)
        return 0

    lax.fori_loop(0, count // chunk, part, 0)


class Reduction:
    orders = (
        (("y", 0), ("y", 1), ("x", 0), ("x", 1), ("z", 0)),
        (("x", 0), ("x", 1), ("y", 0), ("y", 1), ("z", 0)),
    )

    def __init__(self, pos, buf, from_core, from_step, singles, landed, send, recv):
        self.pos, self.buf, self.from_core, self.from_step = pos, buf, from_core, from_step
        self.singles, self.landed = singles, landed
        self.send, self.recv = send, recv

    def core_copy(self):
        return remote(
            self.buf.at[1 - self.pos.core],
            self.from_core,
            self.send.at[0],
            self.recv.at[0],
            self.pos.other_core(),
        )

    def base(self, half, steps):
        start, size = 0, 32
        for axis, step in self.orders[half][:steps]:
            size //= 2
            start = start + self.pos.halving(axis, step)[0] * size
        return start

    def step_copy(self, half, number):
        size = 16 >> number
        keep, partner = self.pos.halving(*self.orders[half][number])
        start = self.base(half, number) + (1 - keep) * size
        sem = 1 + half * 5 + number
        return remote(
            self.buf.at[self.pos.core, half, pl.ds(start, size)],
            self.from_step.at[half, pl.ds(32 - 2 * size, size)],
            self.send.at[sem],
            self.recv.at[sem],
            partner,
        )

    def half_copy(self):
        return remote(
            self.singles.at[1 - self.pos.half],
            self.singles.at[2],
            self.send.at[11],
            self.recv.at[11],
            self.pos.at_far(self.pos.flip(self.pos.far)),
        )

    def last_copy(self):
        return remote(
            self.singles.at[3],
            self.singles.at[4],
            self.send.at[12],
            self.recv.at[12],
            self.pos.at_far(3 - self.pos.far),
        )

    def delivery(self, t):
        return remote(
            self.singles.at[5],
            self.landed.at[self.pos.core, self.pos.half],
            self.send.at[13 + t],
            self.recv.at[13 + self.pos.core * 2 + self.pos.half],
            self.pos.targets()[t],
        )

    def arrival(self, c, h):
        return remote(
            self.singles.at[5],
            self.landed.at[c, h],
            self.send.at[13],
            self.recv.at[13 + c * 2 + h],
            self.pos.sources()[c][h],
        )

    def stage(self, number):
        pos, singles = self.pos, self.singles
        if number == 0:
            self.core_copy().start()
        elif number == 1:
            self.core_copy().wait()
            for half in range(2):
                add_into(self.buf, (pos.core, half), self.from_core.at[half], 0, 32)
                self.step_copy(half, 0).start()
        elif number <= 6:
            for half in range(2):
                self.step_copy(half, number - 2).wait()
                size = 16 >> (number - 2)
                add_into(
                    self.buf,
                    (pos.core, half),
                    self.from_step.at[half, pl.ds(32 - 2 * size, size)],
                    self.base(half, number - 1),
                    size,
                )
                if number <= 5:
                    self.step_copy(half, number - 1).start()
                else:
                    singles[half] = self.buf[pos.core, half, self.base(half, 5)]
            if number == 6:
                self.half_copy().start()
        elif number == 7:
            self.half_copy().wait()
            singles[3] = (singles[pos.half].astype(f32) + singles[2].astype(f32)).astype(bf16)
            self.last_copy().start()
        elif number == 8:
            self.last_copy().wait()
            singles[5] = (singles[3].astype(f32) + singles[4].astype(f32)).astype(bf16)
            for t in range(4):
                self.delivery(t).start()
        else:
            for t in range(4):
                self.delivery(t).wait_send()
            for c in range(2):
                for h in range(2):
                    self.arrival(c, h).wait_recv()


def block_index(core, half, space):
    z, x = space // 4, space % 4
    q, p = ring_place[core][z // 2], ring_place[core][x]
    return (q * 8 + p * 2 + z % 2) if half == 0 else (p * 8 + q * 2 + z % 2)


def kernel(
    feature,
    w1_hbm,
    wd_hbm,
    w2_hbm,
    upstream,
    rule1,
    rule2,
    child,
    send1,
    send2,
    count1,
    count2,
    coarse_out,
    input_grad,
    wide_out,
    thin_out,
    w1,
    wd,
    w2,
    table1,
    halo1,
    pack1,
    picked1,
    act1,
    pickedd,
    actd,
    coarse,
    pack2,
    halo2,
    picked2,
    back2,
    ext_grad2,
    give2,
    take2,
    grad_level,
    back1,
    ext_grad1,
    give1,
    take1,
    strips,
    wide_buf,
    wide_core,
    wide_step,
    wide_singles,
    wide_land,
    thin_buf,
    thin_core,
    thin_step,
    thin_singles,
    thin_land,
    load_sem,
    halo_send,
    halo_recv,
    wide_send,
    wide_recv,
    thin_send,
    thin_recv,
):
    pos = Position()
    greet(pos.partners())
    wide = Reduction(
        pos, wide_buf, wide_core, wide_step, wide_singles, wide_land, wide_send, wide_recv
    )
    thin = Reduction(
        pos, thin_buf, thin_core, thin_step, thin_singles, thin_land, thin_send, thin_recv
    )
    loads = [
        pltpu.make_async_copy(source, target, load_sem.at[i])
        for i, (source, target) in enumerate([(w1_hbm, w1), (wd_hbm, wd), (w2_hbm, w2)])
    ]
    for load in loads:
        load.start()

    def live_rows(rows, counts, width):
        lane = lax.broadcasted_iota(i32, (1, width), 1)
        return jnp.concatenate(
            [jnp.where(lane < counts[d], rows[d : d + 1, :], -1) for d in range(8)], axis=1
        )

    def exchange(number, source, target, sign):
        return [
            remote(
                source(d),
                target(d),
                halo_send.at[number, d],
                halo_recv.at[number, d],
                pos.brick(d, sign),
            )
            for d in range(8)
        ]

    def folded(d):
        return (pl.ds(d // 2 * C1, C1), pl.ds(d % 2 * H1, H1))

    def tap_rows(k, channels):
        return pl.ds(pl.multiple_of(k * channels, channels), channels)

    def fold(target, values):
        for w in range(4):
            target[w * C1 : (w + 1) * C1, :] = values[:, w * 256 : (w + 1) * 256]

    def unfold(values):
        return jnp.concatenate([values[w * C1 : (w + 1) * C1] for w in range(4)], axis=1)

    live1 = live_rows(send1, count1, H1)
    fold(table1, feature[...])
    pack1[...] = gather_four(table1[...], live1, 0)
    await_greetings(pos.partners())
    copies = exchange(
        0, lambda d: pack1.at[:, pl.ds(d * H1, H1)], lambda d: halo1.at[folded(d)], 1
    )
    for copy in copies:
        copy.start()
    strips[...] = jnp.zeros_like(strips)
    picked2[TAPS * C2 :, :] = jnp.zeros((128, C2), bf16)

    def tap_one(k, _):
        picked1[tap_rows(k, C1), :] = gather_four(table1[...], rule1[k], 0)
        return 0

    lax.fori_loop(0, TAPS, tap_one, 0, unroll=9)
    for copy in copies:
        copy.wait()

    def tap_one_halo(k, _):
        here = (tap_rows(k, C1), slice(None))
        picked1[here] = picked1[here] + gather_four(halo1[...], rule1[k], V)
        return 0

    lax.fori_loop(0, TAPS, tap_one_halo, 0, unroll=9)
    loads[0].wait()
    act = dot(w1[...], picked1[...])
    act1[...] = act
    fold(table1, (feature[...].astype(f32) + silu(act)).astype(bf16))

    for m in range(8):
        pickedd[m * C1 : (m + 1) * C1, :] = gather_four(table1[...], child[m : m + 1, :], 0)
    loads[1].wait()
    act = dot(wd[...], pickedd[...])
    actd[...] = act
    coarse[...] = silu(act).astype(bf16)

    live2 = live_rows(send2, count2, H2)
    pack2[...] = dot(coarse[...], one_hot(live2, V2)).T.astype(bf16)
    copies = exchange(
        1, lambda d: pack2.at[pl.ds(d * H2, H2)], lambda d: halo2.at[pl.ds(d * H2, H2)], 1
    )
    for copy in copies:
        copy.start()

    def tap_two(k, _):
        picked2[tap_rows(k, C2), :] = dot(coarse[...], one_hot(rule2[k], V2)).astype(bf16)
        return 0

    lax.fori_loop(0, TAPS, tap_two, 0, unroll=9)
    for copy in copies:
        copy.wait()
    halo2[...] = halo2[...].astype(f32).T.astype(bf16)

    def tap_two_halo(k, _):
        here = (tap_rows(k, C2), slice(None))
        mine = dot(halo2[...], one_hot(rule2[k] - V2, V2)).astype(bf16)
        picked2[here] = picked2[here] + mine
        return 0

    lax.fori_loop(0, TAPS, tap_two_halo, 0, unroll=9)
    loads[2].wait()
    act = dot(w2[...], picked2[: TAPS * C2, :])
    coarse_out[...] = (coarse[...].astype(f32) + silu(act)).astype(bf16)
    grad_two = (upstream[...].astype(f32) * silu_grad(act)).astype(bf16)

    def spread_two(first):
        ext_grad2[...] = jnp.zeros_like(ext_grad2)

        def taps(t, _):
            total = ext_grad2[...]
            for j in range(9):
                k = t * 9 + j
                total += dot_nt(back2[tap_rows(k, C2), :], one_hot(rule2[k] - first, V2))
            ext_grad2[...] = total
            return 0

        lax.fori_loop(0, TAPS // 9, taps, 0)

    back2[...] = dot_tn(w2[...], grad_two).astype(bf16)
    spread_two(V2)
    give2[...] = ext_grad2[...].T.astype(bf16)
    copies = exchange(
        2, lambda d: give2.at[pl.ds(d * H2, H2)], lambda d: take2.at[pl.ds(d * H2, H2)], -1
    )
    for copy in copies:
        copy.start()
    for quarter in range(4):
        core, half = quarter // 2, quarter % 2
        upper = dot_nt(grad_two, picked2[quarter * WIDE : (quarter + 1) * WIDE, :])
        start = TAPS * V2 // 2 + quarter * WIDE
        lower = dot_nt(grad_two, picked2[start : start + WIDE, :])
        both = jnp.concatenate([upper.reshape(32, 8, WIDE), lower.reshape(32, 8, WIDE)], axis=1)
        both = both.astype(bf16)
        for space in range(32):
            wide_buf[core, half, block_index(core, half, space)] = both[space]
    wide.stage(0)
    spread_two(0)
    for copy in copies:
        copy.wait()
    returned = dot(one_hot(live2, V2), take2[...]).T
    grad_coarse = upstream[...].astype(f32) + ext_grad2[...] + returned
    grad_down = (grad_coarse * silu_grad(actd[...])).astype(bf16)

    backd = dot_tn(wd[...], grad_down).astype(bf16)
    total = jnp.zeros((4 * C1, 256), f32)
    for m in range(8):
        total += scatter_four(backd[m * C1 : (m + 1) * C1], child[m : m + 1, :], 0)
    grad_level[...] = total
    wide.stage(1)
    grad_one = (unfold(total) * silu_grad(act1[...])).astype(bf16)
    term_down = dot_nt(grad_down, pickedd[...]).reshape(32, 8, 768)
    term_one = dot_nt(grad_one, picked1[...]).astype(bf16)
    for q in range(5):
        width = min(640, TAPS * C1 - q * 640)
        strips[q * C1 : (q + 1) * C1, :width] = term_one[:, q * 640 : q * 640 + width]
    spot = lax.broadcasted_iota(i32, (1, 5 * C1), 1)
    strip, out_row = spot // C1, spot % C1
    spot = (out_row // 3) * 16 + (out_row % 3) * 5 + strip
    first = dot(one_hot(spot, 512), strips[...]).reshape(32, 16, 640)
    other = jnp.concatenate([term_down[:, :, :384], term_down[:, :, 384:]], axis=1)
    for quarter in range(4):
        core, half = quarter // 2, quarter % 2
        low, high = quarter * THIN, (quarter + 1) * THIN
        if high <= 640:
            both = first[:, :, low:high]
        elif low >= 640:
            both = other[:, :, low - 640 : high - 640]
        else:
            both = jnp.concatenate([first[:, :, low:], other[:, :, : high - 640]], axis=2)
        both = both.astype(bf16)
        for space in range(32):
            thin_buf[core, half, block_index(core, half, space)] = both[space]
    thin.stage(0)

    back1[...] = dot_tn(w1[...], grad_one).astype(bf16)

    def spread_one(first, beside):
        ext_grad1[...] = jnp.zeros_like(ext_grad1)

        def taps(t, _):
            for part, (begin, end) in enumerate(((0, 5), (5, 9))):
                for (when, where), stages in beside.items():
                    if where == part:

                        @pl.when(t == when)
                        def _():
                            for reduction, number in stages:
                                reduction.stage(number)

                total = ext_grad1[...]
                for j in range(begin, end):
                    k = t * 9 + j
                    total += scatter_four(back1[tap_rows(k, C1), :], rule1[k], first)
                ext_grad1[...] = total
            return 0

        lax.fori_loop(0, TAPS // 9, taps, 0)

    spread_one(
        V,
        {
            (0, 0): [(thin, 1), (wide, 2)],
            (1, 0): [(thin, 2), (wide, 3)],
            (2, 0): [(thin, 3), (wide, 4)],
            (2, 1): [(thin, 4)],
        },
    )
    give1[...] = ext_grad1[...].astype(bf16)
    copies = exchange(
        3, lambda d: give1.at[folded(d)], lambda d: take1.at[:, pl.ds(d * H1, H1)], -1
    )
    for copy in copies:
        copy.start()
    spread_one(
        0,
        {
            (0, 0): [(wide, 5), (thin, 5)],
            (0, 1): [(thin, 6)],
            (1, 0): [(wide, 6), (thin, 7)],
            (1, 1): [(thin, 8)],
            (2, 0): [(wide, 7), (thin, 9)],
            (2, 1): [(wide, 8)],
        },
    )
    for copy in copies:
        copy.wait()
    total = grad_level[...] + ext_grad1[...] + scatter_four(take1[...], live1, 0)
    input_grad[...] = unfold(total).astype(bf16)
    thin_out[...] = thin_land[...]
    wide.stage(9)
    wide_out[...] = wide_land[...]


def finish(coarse_in, input_in, wide_in, thin_in, coarse_out, input_grad, gw1, gwd, gw2):
    coarse_out[...] = coarse_in[...]
    input_grad[...] = input_in[...]
    scale = 1.0 / 256
    for quarter in range(4):
        piece = wide_in[quarter // 2, quarter % 2].astype(f32) * scale
        for side in range(2):
            start = quarter * WIDE
            width = min(WIDE, TAPS * V2 // 2 - start)
            here = side * TAPS * V2 // 2 + start
            gw2[:, here : here + width] = piece[side * 8 : side * 8 + 8, :width]
    pieces = [thin_in[q // 2, q % 2].astype(f32) * scale for q in range(4)]
    thin_all = jnp.concatenate(pieces, axis=1)
    gwd[:, :384] = thin_all[:8, 640:]
    gwd[:, 384:] = thin_all[8:, 640:]
    for r in range(3):
        for q in range(5):
            width = min(640, TAPS * C1 - q * 640)
            row = r * 5 + q
            gw1[r : r + 1, q * 640 : q * 640 + width] = thin_all[row : row + 1, :width]


def reduction_scratch(lanes):
    return [
        pltpu.VMEM((2, 2, 32, 16, lanes), bf16),
        pltpu.VMEM((2, 32, 16, lanes), bf16),
        pltpu.VMEM((2, 32, 16, lanes), bf16),
        pltpu.VMEM((6, 16, lanes), bf16),
        pltpu.VMEM((2, 2, 16, lanes), bf16),
    ]


def run_kernels(*operands):
    vmem = pl.BlockSpec(memory_space=pltpu.VMEM)
    smem = pl.BlockSpec(memory_space=pltpu.SMEM)
    away = pl.BlockSpec(memory_space=pl.ANY)
    dma = pltpu.SemaphoreType.DMA
    results = pl.pallas_call(
        kernel,
        out_shape=(
            jax.ShapeDtypeStruct((C2, V2), bf16),
            jax.ShapeDtypeStruct((C1, V), bf16),
            jax.ShapeDtypeStruct((2, 2, 16, WIDE), bf16),
            jax.ShapeDtypeStruct((2, 2, 16, THIN), bf16),
        ),
        in_specs=[vmem] + [away] * 3 + [vmem] * 6 + [smem] * 2,
        out_specs=[vmem] * 4,
        scratch_shapes=[
            pltpu.VMEM((C1, TAPS * C1), bf16),
            pltpu.VMEM((C2, 8 * C1), bf16),
            pltpu.VMEM((C2, TAPS * C2), bf16),
            pltpu.VMEM((4 * C1, 256), bf16),
            pltpu.VMEM((4 * C1, 256), bf16),
            pltpu.VMEM((C1, V), bf16),
            pltpu.VMEM((TAPS * C1, V), bf16),
            pltpu.VMEM((C1, V), f32),
            pltpu.VMEM((8 * C1, V2), bf16),
            pltpu.VMEM((C2, V2), f32),
            pltpu.VMEM((C2, V2), bf16),
            pltpu.VMEM((V2, C2), bf16),
            pltpu.VMEM((V2, C2), bf16),
            pltpu.VMEM((TAPS * C2 + 128, V2), bf16),
            pltpu.VMEM((TAPS * C2, V2), bf16),
            pltpu.VMEM((C2, V2), f32),
            pltpu.VMEM((V2, C2), bf16),
            pltpu.VMEM((V2, C2), bf16),
            pltpu.VMEM((4 * C1, 256), f32),
            pltpu.VMEM((TAPS * C1, V), bf16),
            pltpu.VMEM((4 * C1, 256), f32),
            pltpu.VMEM((4 * C1, 256), bf16),
            pltpu.VMEM((C1, V), bf16),
            pltpu.VMEM((5 * C1, 640), bf16),
            *reduction_scratch(WIDE),
            *reduction_scratch(THIN),
            dma((3,)),
            dma((4, 8)),
            dma((4, 8)),
            dma((17,)),
            dma((17,)),
            dma((17,)),
            dma((17,)),
        ],
        compiler_params=pltpu.CompilerParams(
            collective_id=0, has_side_effects=True, vmem_limit_bytes=58 << 20
        ),
    )(*operands)
    return pl.pallas_call(
        finish,
        out_shape=(
            jax.ShapeDtypeStruct((C2, V2), bf16),
            jax.ShapeDtypeStruct((C1, V), bf16),
            jax.ShapeDtypeStruct((3, TAPS * C1), f32),
            jax.ShapeDtypeStruct((8, 8 * C1), f32),
            jax.ShapeDtypeStruct((8, TAPS * C2), f32),
        ),
        in_specs=[vmem] * 4,
        out_specs=[vmem] * 5,
    )(*results)


def body(
    features,
    weight_one,
    weight_down,
    weight_two,
    cotangent,
    rule_one,
    rule_two,
    children,
    send_one,
    count_one,
    send_two,
    count_two,
):
    coarse_out, input_grad, gw1, gwd, gw2 = run_kernels(
        features[0],
        weight_one,
        weight_down,
        weight_two,
        cotangent[0],
        rule_one.transpose(1, 0, 2),
        rule_two.transpose(1, 0, 2),
        children[0],
        send_one[0, 0],
        send_two[0, 0],
        count_one[0, 0],
        count_two[0, 0],
    )
    return coarse_out[None], input_grad[None], gw1, gwd, gw2


def solution(mesh):
    tile = P("dp", None, "space")
    brick = P("dp", "space", None, None)
    count = P("dp", "space", None)
    return jax.shard_map(
        body,
        mesh=mesh,
        in_specs=(tile, P(), P(), P(), tile, tile, tile, tile, brick, count, brick, count),
        out_specs=(tile, tile, P("space", None), P("space", None), P("space", None)),
        check_vma=False,
    )
```

```python
import jax
import jax.numpy as jnp
from jax import lax
from jax.experimental import pallas as pl
from jax.experimental.pallas import tpu as pltpu
from jax.sharding import PartitionSpec as P

bf16 = jnp.bfloat16
f32 = jnp.float32
i32 = jnp.int32
C1, C2, V, V2, H1, H2, TAPS = 96, 256, 1024, 256, 128, 32, 27
WIDE = 896
WINDOW = 512
THIN = 256
directions = ((-1, -1), (-1, 0), (-1, 1), (0, -1), (0, 1), (1, -1), (1, 0), (1, 1))
ring_place = ((0, 2, 3, 1), (0, 1, 3, 2))


def dot(a, b):
    return jnp.dot(a, b, preferred_element_type=f32)


def dot_nt(a, b):
    return lax.dot_general(a, b, (((1,), (1,)), ((), ())), preferred_element_type=f32)


def dot_tn(a, b):
    return lax.dot_general(a, b, (((0,), (0,)), ((), ())), preferred_element_type=f32)


def one_hot(row, size):
    return jnp.where(
        lax.broadcasted_iota(jnp.int16, (size, row.shape[1]), 0) == row.astype(jnp.int16),
        jnp.ones((), bf16),
        jnp.zeros((), bf16),
    )


def logistic(v):
    return 1.0 / (1.0 + jnp.exp(-v))


def silu(v):
    return v * logistic(v)


def silu_grad(v):
    s = logistic(v)
    return s * (1.0 + v * (1.0 - s))


def place():
    return lax.axis_index("dp"), lax.axis_index("space")


def remote(src, dst, send_sem, recv_sem, device):
    return pltpu.make_async_remote_copy(
        src_ref=src,
        dst_ref=dst,
        send_sem=send_sem,
        recv_sem=recv_sem,
        device_id=device,
        device_id_type=pl.DeviceIdType.MESH,
    )


def greet(pos):
    barrier = pltpu.get_barrier_semaphore()
    mesh_id = pl.DeviceIdType.MESH
    for device in pos.partners():
        pl.semaphore_signal(barrier, inc=1, device_id=device, device_id_type=mesh_id)
    for core in range(2):
        for far in range(4):

            @pl.when(jnp.logical_not(pos.own_rows() & (pos.core == core) & (pos.far == far)))
            def _():
                holder = pos.holder(core, far)
                pl.semaphore_signal(barrier, inc=1, device_id=holder, device_id_type=mesh_id)


def await_greetings(pos):
    own = jnp.where(pos.own_rows(), 1, 0)
    pl.semaphore_wait(pltpu.get_barrier_semaphore(), len(pos.partners()) + 8 - own)


def in_table(row, first):
    return jnp.where((row >= first) & (row < first + V), row & 255, -1)


def gather_four(table, row, first):
    both = dot(table, one_hot(in_table(row, first), 256))
    odd, upper = (row & 256) != 0, (row & 512) != 0
    low = jnp.where(odd, both[C1 : 2 * C1], both[:C1])
    high = jnp.where(odd, both[3 * C1 :], both[2 * C1 : 3 * C1])
    return jnp.where(upper, high, low).astype(bf16)


def scatter_four(values, row, first):
    place_four = (row >> 8) & 3
    zero = jnp.zeros_like(values)
    spread = jnp.concatenate(
        [jnp.where(place_four == w, values, zero) for w in range(4)], axis=0
    )
    return dot_nt(spread, one_hot(in_table(row, first), 256))


class Position:
    def __init__(self):
        self.dp, self.space = place()
        self.y, self.core = self.dp // 2, self.dp % 2
        self.z, self.x = self.space // 4, self.space % 4
        self.far, self.near = self.z // 2, self.z % 2

    def brick(self, direction, sign):
        dy, dx = directions[direction]
        gy = (self.space // 8 + sign * dy + 4) % 4
        gx = (self.space % 8 + sign * dx + 8) % 8
        return (self.dp, gy * 8 + gx)

    def other_core(self):
        return (self.y * 2 + 1 - self.core, self.space)

    def at_y(self, y):
        return (y * 2 + self.core, self.space)

    def at_x(self, x):
        return (self.dp, self.z * 4 + x)

    def at_z(self, z):
        return (self.dp, z * 4 + self.x)

    def at_far(self, far):
        return self.at_z(far * 2 + self.near)

    def gray(self, v):
        return (v + v // 2) % 2

    def flip(self, v):
        return v + 1 - 2 * (v % 2)

    def halving(self, axis, step):
        v, at = (self.y, self.at_y) if axis == "y" else (self.x, self.at_x)
        first = 1 - self.core if step == 0 else self.core
        keep = first * self.gray(v) + (1 - first) * (v // 2)
        return keep, at(first * self.flip(v) + (1 - first) * (3 - v))

    def at_axis(self, axis, offset):
        if axis == "y":
            return self.at_y((self.y + offset) % 4)
        return self.at_x((self.x + offset) % 4)

    def holder(self, core, far):
        return (self.far * 2 + core, (far * 2 + self.near) * 4 + self.x)

    def target(self, offset):
        return ((self.dp + offset) % 8, (self.y * 2 + self.near) * 4 + self.x)

    def own_rows(self):
        return self.far == self.y

    def partners(self):
        return (
            [self.brick(d, 1) for d in range(8)]
            + [self.other_core()]
            + [self.at_axis(axis, offset) for axis in "yx" for offset in range(1, 4)]
            + [self.at_z((self.z + offset) % 8) for offset in (1, 3, 4, 5, 7)]
        )


def add_into(target, index, source, start, count):
    chunk = min(count, 4)

    def part(i, _):
        here = index + (pl.ds(start + i * chunk, chunk),)
        total = target[here].astype(f32) + source[pl.ds(i * chunk, chunk)].astype(f32)
        target[here] = total.astype(bf16)
        return 0

    lax.fori_loop(0, count // chunk, part, 0)


class Reduction:
    axes = ("yx", "xy")

    def __init__(self, pos, window, shift, refs, send, recv):
        self.pos, self.window, self.shift = pos, window, shift
        self.buf, self.from_core, self.from_step, self.from_axis = refs[:4]
        self.parts, self.from_z, self.total, self.landed = refs[4:]
        self.send, self.recv = send, recv

    def copy(self, source, target, sem, device):
        return remote(source, target, self.send.at[sem], self.recv.at[sem], device)

    def core_copy(self):
        pos = self.pos
        return self.copy(self.buf.at[1 - pos.core], self.from_core, 0, pos.other_core())

    def base(self, half, steps):
        start, size = 0, 32
        for step in range(steps):
            size //= 2
            start = start + self.pos.halving(self.axes[half][0], step)[0] * size
        return start

    def step_copy(self, half, step):
        size = 16 >> step
        keep, partner = self.pos.halving(self.axes[half][0], step)
        start = self.base(half, step) + (1 - keep) * size
        return self.copy(
            self.buf.at[self.pos.core, half, pl.ds(start, size)],
            self.from_step.at[half, pl.ds(32 - 2 * size, size)],
            1 + half * 2 + step,
            partner,
        )

    def axis_block(self, half, offset):
        v = self.pos.x if half == 0 else self.pos.y
        return self.base(half, 2) + (v + offset) % 4 * 2

    def axis_copy(self, half, offset):
        return self.copy(
            self.buf.at[self.pos.core, half, pl.ds(self.axis_block(half, offset), 2)],
            self.from_axis.at[half, offset - 1],
            4 + half * 3 + offset,
            self.pos.at_axis(self.axes[half][1], offset),
        )

    def z_copy(self, offset):
        z = (self.pos.z + offset) % 8
        return self.copy(
            self.parts.at[z], self.from_z.at[offset - 1], 10 + offset, self.pos.at_z(z)
        )

    def delivery(self, offset):
        pos = self.pos
        return remote(
            self.total,
            self.landed.at[pos.core, pos.far],
            self.send.at[18 + offset],
            self.recv.at[18 + pos.core * 4 + pos.far],
            pos.target(offset),
        )

    def own_delivery(self):
        pos = self.pos
        return pltpu.make_async_copy(
            self.total, self.landed.at[pos.core, pos.far], self.send.at[18]
        )

    def arrival(self, core, far):
        return remote(
            self.total,
            self.landed.at[core, far],
            self.send.at[18],
            self.recv.at[18 + core * 4 + far],
            self.pos.holder(core, far),
        )

    def finish_step(self, step):
        size = 16 >> step
        for half in range(2):
            self.step_copy(half, step).wait()
            add_into(
                self.buf,
                (self.pos.core, half),
                self.from_step.at[half, pl.ds(32 - 2 * size, size)],
                self.base(half, step + 1),
                size,
            )
            if step == 0:
                self.step_copy(half, 1).start()
            else:
                for offset in range(1, 4):
                    self.axis_copy(half, offset).start()

    def stage(self, number):
        pos = self.pos
        if number == 0:
            self.core_copy().start()
        elif number == 1:
            self.core_copy().wait()
            for half in range(2):
                add_into(self.buf, (pos.core, half), self.from_core.at[half], 0, 32)
                self.step_copy(half, 0).start()
        elif number <= 3:
            self.finish_step(number - 2)
        elif number == 4:
            for half in range(2):
                for offset in range(1, 4):
                    self.axis_copy(half, offset).wait()
                own = self.buf[pos.core, half, pl.ds(self.axis_block(half, 0), 2)].astype(f32)
                for offset in range(3):
                    own = own + self.from_axis[half, offset].astype(f32)
                own = own.astype(bf16)
                for sub in range(2):
                    lanes = slice(sub * self.shift, sub * self.shift + self.window)
                    for near in range(2):
                        self.parts[(half * 2 + sub) * 2 + near] = own[near, :, lanes]
            for offset in range(1, 8):
                self.z_copy(offset).start()
        elif number == 5:
            for offset in range(1, 8):
                self.z_copy(offset).wait()
            total = self.parts[pos.z].astype(f32)
            for offset in range(7):
                total = total + self.from_z[offset].astype(f32)
            self.total[...] = total.astype(bf16)
            for offset in range(1, 8):
                self.delivery(offset).start()

            @pl.when(pos.own_rows())
            def _():
                self.own_delivery().start()

            @pl.when(jnp.logical_not(pos.own_rows()))
            def _():
                self.delivery(0).start()

        else:
            for offset in range(1, 8):
                self.delivery(offset).wait_send()

            @pl.when(pos.own_rows())
            def _():
                self.own_delivery().wait()

            @pl.when(jnp.logical_not(pos.own_rows()))
            def _():
                self.delivery(0).wait_send()

            for core in range(2):
                for far in range(4):
                    own = pos.own_rows() & (pos.core == core) & (pos.far == far)

                    @pl.when(jnp.logical_not(own))
                    def _():
                        self.arrival(core, far).wait_recv()


def block_index(core, half, space):
    z, x = space // 4, space % 4
    if half == 0:
        return ring_place[core][z // 2] * 8 + x * 2 + z % 2
    return ring_place[core][x] * 8 + z // 2 * 2 + z % 2


def kernel(
    feature,
    w1_hbm,
    wd_hbm,
    w2_hbm,
    upstream,
    rule1,
    rule2,
    child,
    send1,
    send2,
    count1,
    count2,
    coarse_out,
    input_grad,
    wide_out,
    thin_out,
    w1,
    wd,
    w2,
    table1,
    halo1,
    pack1,
    picked1,
    act1,
    pickedd,
    actd,
    coarse,
    pack2,
    halo2,
    picked2,
    back2,
    ext_grad2,
    give2,
    take2,
    grad_level,
    back1,
    ext_grad1,
    give1,
    take1,
    strips,
    wide_buf,
    wide_core,
    wide_step,
    wide_axis,
    wide_parts,
    wide_z,
    wide_total,
    wide_land,
    thin_buf,
    thin_core,
    thin_step,
    thin_axis,
    thin_parts,
    thin_z,
    thin_total,
    thin_land,
    load_sem,
    halo_send,
    halo_recv,
    wide_send,
    wide_recv,
    thin_send,
    thin_recv,
):
    pos = Position()
    greet(pos)
    wide_refs = (wide_buf, wide_core, wide_step, wide_axis, wide_parts, wide_z, wide_total, wide_land)
    thin_refs = (thin_buf, thin_core, thin_step, thin_axis, thin_parts, thin_z, thin_total, thin_land)
    wide = Reduction(pos, WINDOW, WIDE - WINDOW, wide_refs, wide_send, wide_recv)
    thin = Reduction(pos, THIN // 2, THIN // 2, thin_refs, thin_send, thin_recv)
    loads = [
        pltpu.make_async_copy(source, target, load_sem.at[i])
        for i, (source, target) in enumerate([(w1_hbm, w1), (wd_hbm, wd), (w2_hbm, w2)])
    ]
    for load in loads:
        load.start()

    def live_rows(rows, counts, width):
        lane = lax.broadcasted_iota(i32, (1, width), 1)
        return jnp.concatenate(
            [jnp.where(lane < counts[d], rows[d : d + 1, :], -1) for d in range(8)], axis=1
        )

    def exchange(number, source, target, sign):
        return [
            remote(
                source(d),
                target(d),
                halo_send.at[number, d],
                halo_recv.at[number, d],
                pos.brick(d, sign),
            )
            for d in range(8)
        ]

    def folded(d):
        return (pl.ds(d // 2 * C1, C1), pl.ds(d % 2 * H1, H1))

    def tap_rows(k, channels):
        return pl.ds(pl.multiple_of(k * channels, channels), channels)

    def fold(target, values):
        for w in range(4):
            target[w * C1 : (w + 1) * C1, :] = values[:, w * 256 : (w + 1) * 256]

    def unfold(values):
        return jnp.concatenate([values[w * C1 : (w + 1) * C1] for w in range(4)], axis=1)

    live1 = live_rows(send1, count1, H1)
    fold(table1, feature[...])
    pack1[...] = gather_four(table1[...], live1, 0)
    await_greetings(pos)
    copies = exchange(
        0, lambda d: pack1.at[:, pl.ds(d * H1, H1)], lambda d: halo1.at[folded(d)], 1
    )
    for copy in copies:
        copy.start()
    strips[...] = jnp.zeros_like(strips)
    picked2[TAPS * C2 :, :] = jnp.zeros((128, C2), bf16)

    def tap_one(k, _):
        picked1[tap_rows(k, C1), :] = gather_four(table1[...], rule1[k], 0)
        return 0

    lax.fori_loop(0, TAPS, tap_one, 0, unroll=9)
    for copy in copies:
        copy.wait()

    def tap_one_halo(k, _):
        here = (tap_rows(k, C1), slice(None))
        picked1[here] = picked1[here] + gather_four(halo1[...], rule1[k], V)
        return 0

    lax.fori_loop(0, TAPS, tap_one_halo, 0, unroll=9)
    loads[0].wait()
    act = dot(w1[...], picked1[...])
    act1[...] = act
    fold(table1, (feature[...].astype(f32) + silu(act)).astype(bf16))

    for m in range(8):
        pickedd[m * C1 : (m + 1) * C1, :] = gather_four(table1[...], child[m : m + 1, :], 0)
    loads[1].wait()
    act = dot(wd[...], pickedd[...])
    actd[...] = act
    coarse[...] = silu(act).astype(bf16)

    live2 = live_rows(send2, count2, H2)
    pack2[...] = dot(coarse[...], one_hot(live2, V2)).T.astype(bf16)
    copies = exchange(
        1, lambda d: pack2.at[pl.ds(d * H2, H2)], lambda d: halo2.at[pl.ds(d * H2, H2)], 1
    )
    for copy in copies:
        copy.start()

    def tap_two(k, _):
        picked2[tap_rows(k, C2), :] = dot(coarse[...], one_hot(rule2[k], V2)).astype(bf16)
        return 0

    lax.fori_loop(0, TAPS, tap_two, 0, unroll=9)
    for copy in copies:
        copy.wait()
    halo2[...] = halo2[...].astype(f32).T.astype(bf16)

    def tap_two_halo(k, _):
        here = (tap_rows(k, C2), slice(None))
        mine = dot(halo2[...], one_hot(rule2[k] - V2, V2)).astype(bf16)
        picked2[here] = picked2[here] + mine
        return 0

    lax.fori_loop(0, TAPS, tap_two_halo, 0, unroll=9)
    loads[2].wait()
    act = dot(w2[...], picked2[: TAPS * C2, :])
    coarse_out[...] = (coarse[...].astype(f32) + silu(act)).astype(bf16)
    grad_two = (upstream[...].astype(f32) * silu_grad(act)).astype(bf16)

    def spread_two(first):
        ext_grad2[...] = jnp.zeros_like(ext_grad2)

        def taps(t, _):
            total = ext_grad2[...]
            for j in range(9):
                k = t * 9 + j
                total += dot_nt(back2[tap_rows(k, C2), :], one_hot(rule2[k] - first, V2))
            ext_grad2[...] = total
            return 0

        lax.fori_loop(0, TAPS // 9, taps, 0)

    back2[...] = dot_tn(w2[...], grad_two).astype(bf16)
    spread_two(V2)
    give2[...] = ext_grad2[...].T.astype(bf16)
    copies = exchange(
        2, lambda d: give2.at[pl.ds(d * H2, H2)], lambda d: take2.at[pl.ds(d * H2, H2)], -1
    )
    for copy in copies:
        copy.start()
    for quarter in range(4):
        core, half = quarter // 2, quarter % 2
        upper = dot_nt(grad_two, picked2[quarter * WIDE : (quarter + 1) * WIDE, :])
        start = TAPS * V2 // 2 + quarter * WIDE
        lower = dot_nt(grad_two, picked2[start : start + WIDE, :])
        both = jnp.concatenate([upper.reshape(32, 8, WIDE), lower.reshape(32, 8, WIDE)], axis=1)
        both = both.astype(bf16)
        for space in range(32):
            wide_buf[core, half, block_index(core, half, space)] = both[space]
    wide.stage(0)
    spread_two(0)
    wide.stage(1)
    for copy in copies:
        copy.wait()
    returned = dot(one_hot(live2, V2), take2[...]).T
    grad_coarse = upstream[...].astype(f32) + ext_grad2[...] + returned
    grad_down = (grad_coarse * silu_grad(actd[...])).astype(bf16)

    backd = dot_tn(wd[...], grad_down).astype(bf16)
    total = jnp.zeros((4 * C1, 256), f32)
    for m in range(8):
        total += scatter_four(backd[m * C1 : (m + 1) * C1], child[m : m + 1, :], 0)
    grad_level[...] = total
    grad_one = (unfold(total) * silu_grad(act1[...])).astype(bf16)
    term_down = dot_nt(grad_down, pickedd[...]).reshape(32, 8, 768)
    term_one = dot_nt(grad_one, picked1[...]).astype(bf16)
    for q in range(5):
        width = min(640, TAPS * C1 - q * 640)
        strips[q * C1 : (q + 1) * C1, :width] = term_one[:, q * 640 : q * 640 + width]
    spot = lax.broadcasted_iota(i32, (1, 5 * C1), 1)
    strip, out_row = spot // C1, spot % C1
    spot = (out_row // 3) * 16 + (out_row % 3) * 5 + strip
    first = dot(one_hot(spot, 512), strips[...]).reshape(32, 16, 640)
    other = jnp.concatenate([term_down[:, :, :384], term_down[:, :, 384:]], axis=1)
    for quarter in range(4):
        core, half = quarter // 2, quarter % 2
        low, high = quarter * THIN, (quarter + 1) * THIN
        if high <= 640:
            both = first[:, :, low:high]
        elif low >= 640:
            both = other[:, :, low - 640 : high - 640]
        else:
            both = jnp.concatenate([first[:, :, low:], other[:, :, : high - 640]], axis=2)
        both = both.astype(bf16)
        for space in range(32):
            thin_buf[core, half, block_index(core, half, space)] = both[space]
    thin.stage(0)
    wide.stage(2)

    back1[...] = dot_tn(w1[...], grad_one).astype(bf16)

    def spread_one(first, beside):
        ext_grad1[...] = jnp.zeros_like(ext_grad1)

        def taps(t, _):
            for part, (begin, end) in enumerate(((0, 5), (5, 9))):
                for (when, where), stages in beside.items():
                    if where == part:

                        @pl.when(t == when)
                        def _():
                            for reduction, number in stages:
                                reduction.stage(number)

                total = ext_grad1[...]
                for j in range(begin, end):
                    k = t * 9 + j
                    total += scatter_four(back1[tap_rows(k, C1), :], rule1[k], first)
                ext_grad1[...] = total
            return 0

        lax.fori_loop(0, TAPS // 9, taps, 0)

    spread_one(
        V,
        {(0, 1): [(thin, 1)], (1, 1): [(wide, 3)], (2, 0): [(thin, 2)]},
    )
    give1[...] = ext_grad1[...].astype(bf16)
    copies = exchange(
        3, lambda d: give1.at[folded(d)], lambda d: take1.at[:, pl.ds(d * H1, H1)], -1
    )
    for copy in copies:
        copy.start()
    spread_one(
        0,
        {
            (0, 0): [(thin, 3)],
            (0, 1): [(wide, 4)],
            (1, 1): [(thin, 4)],
            (2, 1): [(wide, 5)],
        },
    )
    thin.stage(5)
    for copy in copies:
        copy.wait()
    total = grad_level[...] + ext_grad1[...] + scatter_four(take1[...], live1, 0)
    input_grad[...] = unfold(total).astype(bf16)
    thin.stage(6)
    wide.stage(6)
    thin_out[...] = thin_land[...]
    wide_out[...] = wide_land[...]


def finish(coarse_in, input_in, wide_in, thin_in, coarse_out, input_grad, gw1, gwd, gw2):
    coarse_out[...] = coarse_in[...]
    input_grad[...] = input_in[...]
    scale = 1.0 / 256
    for quarter in range(4):
        core, half = quarter // 2, quarter % 2
        low, high = wide_in[core, half * 2], wide_in[core, half * 2 + 1]
        piece = jnp.concatenate([low, high[:, 2 * WINDOW - WIDE :]], axis=1).astype(f32) * scale
        for side in range(2):
            start = quarter * WIDE
            width = min(WIDE, TAPS * V2 // 2 - start)
            here = side * TAPS * V2 // 2 + start
            gw2[:, here : here + width] = piece[side * 8 : side * 8 + 8, :width]
    pieces = [thin_in[q // 4, q % 4].astype(f32) * scale for q in range(8)]
    thin_all = jnp.concatenate(pieces, axis=1)
    gwd[:, :384] = thin_all[:8, 640:]
    gwd[:, 384:] = thin_all[8:, 640:]
    for r in range(3):
        for q in range(5):
            width = min(640, TAPS * C1 - q * 640)
            row = r * 5 + q
            gw1[r : r + 1, q * 640 : q * 640 + width] = thin_all[row : row + 1, :width]


def reduction_scratch(lanes, window):
    return [
        pltpu.VMEM((2, 2, 32, 16, lanes), bf16),
        pltpu.VMEM((2, 32, 16, lanes), bf16),
        pltpu.VMEM((2, 24, 16, lanes), bf16),
        pltpu.VMEM((2, 3, 2, 16, lanes), bf16),
        pltpu.VMEM((8, 16, window), bf16),
        pltpu.VMEM((7, 16, window), bf16),
        pltpu.VMEM((16, window), bf16),
        pltpu.VMEM((2, 4, 16, window), bf16),
    ]


def run_kernels(*operands):
    vmem = pl.BlockSpec(memory_space=pltpu.VMEM)
    smem = pl.BlockSpec(memory_space=pltpu.SMEM)
    away = pl.BlockSpec(memory_space=pl.ANY)
    dma = pltpu.SemaphoreType.DMA
    results = pl.pallas_call(
        kernel,
        out_shape=(
            jax.ShapeDtypeStruct((C2, V2), bf16),
            jax.ShapeDtypeStruct((C1, V), bf16),
            jax.ShapeDtypeStruct((2, 4, 16, WINDOW), bf16),
            jax.ShapeDtypeStruct((2, 4, 16, THIN // 2), bf16),
        ),
        in_specs=[vmem] + [away] * 3 + [vmem] * 6 + [smem] * 2,
        out_specs=[vmem] * 4,
        scratch_shapes=[
            pltpu.VMEM((C1, TAPS * C1), bf16),
            pltpu.VMEM((C2, 8 * C1), bf16),
            pltpu.VMEM((C2, TAPS * C2), bf16),
            pltpu.VMEM((4 * C1, 256), bf16),
            pltpu.VMEM((4 * C1, 256), bf16),
            pltpu.VMEM((C1, V), bf16),
            pltpu.VMEM((TAPS * C1, V), bf16),
            pltpu.VMEM((C1, V), f32),
            pltpu.VMEM((8 * C1, V2), bf16),
            pltpu.VMEM((C2, V2), f32),
            pltpu.VMEM((C2, V2), bf16),
            pltpu.VMEM((V2, C2), bf16),
            pltpu.VMEM((V2, C2), bf16),
            pltpu.VMEM((TAPS * C2 + 128, V2), bf16),
            pltpu.VMEM((TAPS * C2, V2), bf16),
            pltpu.VMEM((C2, V2), f32),
            pltpu.VMEM((V2, C2), bf16),
            pltpu.VMEM((V2, C2), bf16),
            pltpu.VMEM((4 * C1, 256), f32),
            pltpu.VMEM((TAPS * C1, V), bf16),
            pltpu.VMEM((4 * C1, 256), f32),
            pltpu.VMEM((4 * C1, 256), bf16),
            pltpu.VMEM((C1, V), bf16),
            pltpu.VMEM((5 * C1, 640), bf16),
            *reduction_scratch(WIDE, WINDOW),
            *reduction_scratch(THIN, THIN // 2),
            dma((3,)),
            dma((4, 8)),
            dma((4, 8)),
            dma((26,)),
            dma((26,)),
            dma((26,)),
            dma((26,)),
        ],
        compiler_params=pltpu.CompilerParams(
            collective_id=0, has_side_effects=True, vmem_limit_bytes=58 << 20
        ),
    )(*operands)
    return pl.pallas_call(
        finish,
        out_shape=(
            jax.ShapeDtypeStruct((C2, V2), bf16),
            jax.ShapeDtypeStruct((C1, V), bf16),
            jax.ShapeDtypeStruct((3, TAPS * C1), f32),
            jax.ShapeDtypeStruct((8, 8 * C1), f32),
            jax.ShapeDtypeStruct((8, TAPS * C2), f32),
        ),
        in_specs=[vmem] * 4,
        out_specs=[vmem] * 5,
    )(*results)


def body(
    features,
    weight_one,
    weight_down,
    weight_two,
    cotangent,
    rule_one,
    rule_two,
    children,
    send_one,
    count_one,
    send_two,
    count_two,
):
    coarse_out, input_grad, gw1, gwd, gw2 = run_kernels(
        features[0],
        weight_one,
        weight_down,
        weight_two,
        cotangent[0],
        rule_one.transpose(1, 0, 2),
        rule_two.transpose(1, 0, 2),
        children[0],
        send_one[0, 0],
        send_two[0, 0],
        count_one[0, 0],
        count_two[0, 0],
    )
    return coarse_out[None], input_grad[None], gw1, gwd, gw2


def solution(mesh):
    tile = P("dp", None, "space")
    brick = P("dp", "space", None, None)
    count = P("dp", "space", None)
    return jax.shard_map(
        body,
        mesh=mesh,
        in_specs=(tile, P(), P(), P(), tile, tile, tile, tile, brick, count, brick, count),
        out_specs=(tile, tile, P("space", None), P("space", None), P("space", None)),
        check_vma=False,
    )
```

```python
import jax
import jax.numpy as jnp
from jax import lax
from jax.experimental import pallas as pl
from jax.experimental.pallas import tpu as pltpu
from jax.sharding import PartitionSpec as P

bf16 = jnp.bfloat16
f32 = jnp.float32
i32 = jnp.int32
C1, C2, V, V2, H1, H2, TAPS = 96, 256, 1024, 256, 128, 32, 27
WIDE = 896
WINDOW = 512
THIN = 256
directions = ((-1, -1), (-1, 0), (-1, 1), (0, -1), (0, 1), (1, -1), (1, 0), (1, 1))
ring_place = ((0, 2, 3, 1), (0, 1, 3, 2))


def dot(a, b):
    return jnp.dot(a, b, preferred_element_type=f32)


def dot_nt(a, b):
    return lax.dot_general(a, b, (((1,), (1,)), ((), ())), preferred_element_type=f32)


def dot_tn(a, b):
    return lax.dot_general(a, b, (((0,), (0,)), ((), ())), preferred_element_type=f32)


def one_hot(row, size):
    return jnp.where(
        lax.broadcasted_iota(jnp.int16, (size, row.shape[1]), 0) == row.astype(jnp.int16),
        jnp.ones((), bf16),
        jnp.zeros((), bf16),
    )


def logistic(v):
    return 1.0 / (1.0 + jnp.exp(-v))


def silu(v):
    return v * logistic(v)


def silu_grad(v):
    s = logistic(v)
    return s * (1.0 + v * (1.0 - s))


def place():
    return lax.axis_index("dp"), lax.axis_index("space")


def remote(src, dst, send_sem, recv_sem, device):
    return pltpu.make_async_remote_copy(
        src_ref=src,
        dst_ref=dst,
        send_sem=send_sem,
        recv_sem=recv_sem,
        device_id=device,
        device_id_type=pl.DeviceIdType.MESH,
    )


def greet(pos):
    barrier = pltpu.get_barrier_semaphore()
    mesh_id = pl.DeviceIdType.MESH
    for device in pos.partners():
        pl.semaphore_signal(barrier, inc=1, device_id=device, device_id_type=mesh_id)
    for core in range(2):
        for far in range(4):

            @pl.when(jnp.logical_not(pos.own_rows() & (pos.core == core) & (pos.far == far)))
            def _():
                holder = pos.holder(core, far)
                pl.semaphore_signal(barrier, inc=1, device_id=holder, device_id_type=mesh_id)


def await_greetings(pos):
    own = jnp.where(pos.own_rows(), 1, 0)
    pl.semaphore_wait(pltpu.get_barrier_semaphore(), len(pos.partners()) + 8 - own)


def in_table(row, first):
    return jnp.where((row >= first) & (row < first + V), row & 255, -1)


def gather_four(table, row, first):
    both = dot(table, one_hot(in_table(row, first), 256))
    odd, upper = (row & 256) != 0, (row & 512) != 0
    low = jnp.where(odd, both[C1 : 2 * C1], both[:C1])
    high = jnp.where(odd, both[3 * C1 :], both[2 * C1 : 3 * C1])
    return jnp.where(upper, high, low).astype(bf16)


def scatter_four(values, row, first):
    place_four = (row >> 8) & 3
    zero = jnp.zeros_like(values)
    spread = jnp.concatenate(
        [jnp.where(place_four == w, values, zero) for w in range(4)], axis=0
    )
    return dot_nt(spread, one_hot(in_table(row, first), 256))


class Position:
    def __init__(self):
        self.dp, self.space = place()
        self.y, self.core = self.dp // 2, self.dp % 2
        self.z, self.x = self.space // 4, self.space % 4
        self.far, self.near = self.z // 2, self.z % 2

    def brick(self, direction, sign):
        dy, dx = directions[direction]
        gy = (self.space // 8 + sign * dy + 4) % 4
        gx = (self.space % 8 + sign * dx + 8) % 8
        return (self.dp, gy * 8 + gx)

    def other_core(self):
        return (self.y * 2 + 1 - self.core, self.space)

    def at_y(self, y):
        return (y * 2 + self.core, self.space)

    def at_x(self, x):
        return (self.dp, self.z * 4 + x)

    def at_z(self, z):
        return (self.dp, z * 4 + self.x)

    def at_far(self, far):
        return self.at_z(far * 2 + self.near)

    def gray(self, v):
        return (v + v // 2) % 2

    def flip(self, v):
        return v + 1 - 2 * (v % 2)

    def halving(self, axis, step):
        v, at = (self.y, self.at_y) if axis == "y" else (self.x, self.at_x)
        first = 1 - self.core if step == 0 else self.core
        keep = first * self.gray(v) + (1 - first) * (v // 2)
        return keep, at(first * self.flip(v) + (1 - first) * (3 - v))

    def at_axis(self, axis, offset):
        if axis == "y":
            return self.at_y((self.y + offset) % 4)
        return self.at_x((self.x + offset) % 4)

    def holder(self, core, far):
        return (self.far * 2 + core, (far * 2 + self.near) * 4 + self.x)

    def target(self, offset):
        return ((self.dp + offset) % 8, (self.y * 2 + self.near) * 4 + self.x)

    def own_rows(self):
        return self.far == self.y

    def partners(self):
        return (
            [self.brick(d, 1) for d in range(8)]
            + [self.other_core()]
            + [self.at_axis(axis, offset) for axis in "yx" for offset in range(1, 4)]
            + [self.at_z((self.z + offset) % 8) for offset in (1, 3, 4, 5, 7)]
        )


def add_into(target, index, source, start, count):
    def part(i, size):
        here = index + (pl.ds(start + i, size),)
        total = target[here].astype(f32) + source[pl.ds(i, size)].astype(f32)
        target[here] = total.astype(bf16)

    if count <= 8:
        part(0, count)
        return

    def parts(i, _):
        part(i * 4, 4)
        return 0

    lax.fori_loop(0, count // 4, parts, 0)


class Reduction:
    axes = ("yx", "xy")

    def __init__(self, pos, window, shift, refs, send, recv):
        self.pos, self.window, self.shift = pos, window, shift
        self.buf, self.from_core, self.from_step, self.from_axis = refs[:4]
        self.parts, self.from_z, self.total, self.landed = refs[4:]
        self.send, self.recv = send, recv

    def copy(self, source, target, sem, device):
        return remote(source, target, self.send.at[sem], self.recv.at[sem], device)

    def core_copy(self):
        pos = self.pos
        return self.copy(self.buf.at[1 - pos.core], self.from_core, 0, pos.other_core())

    def base(self, half, steps):
        start, size = 0, 32
        for step in range(steps):
            size //= 2
            start = start + self.pos.halving(self.axes[half][0], step)[0] * size
        return start

    def step_copy(self, half, step):
        size = 16 >> step
        keep, partner = self.pos.halving(self.axes[half][0], step)
        start = self.base(half, step) + (1 - keep) * size
        return self.copy(
            self.buf.at[self.pos.core, half, pl.ds(start, size)],
            self.from_step.at[half, pl.ds(32 - 2 * size, size)],
            1 + half * 2 + step,
            partner,
        )

    def axis_block(self, half, offset):
        v = self.pos.x if half == 0 else self.pos.y
        return self.base(half, 2) + (v + offset) % 4 * 2

    def axis_copy(self, half, offset):
        return self.copy(
            self.buf.at[self.pos.core, half, pl.ds(self.axis_block(half, offset), 2)],
            self.from_axis.at[half, offset - 1],
            4 + half * 3 + offset,
            self.pos.at_axis(self.axes[half][1], offset),
        )

    def z_copy(self, offset):
        z = (self.pos.z + offset) % 8
        return self.copy(
            self.parts.at[z], self.from_z.at[offset - 1], 10 + offset, self.pos.at_z(z)
        )

    def delivery(self, offset):
        pos = self.pos
        return remote(
            self.total,
            self.landed.at[pos.core, pos.far],
            self.send.at[18 + offset],
            self.recv.at[18 + pos.core * 4 + pos.far],
            pos.target(offset),
        )

    def own_delivery(self):
        pos = self.pos
        return pltpu.make_async_copy(
            self.total, self.landed.at[pos.core, pos.far], self.send.at[18]
        )

    def arrival(self, core, far):
        return remote(
            self.total,
            self.landed.at[core, far],
            self.send.at[18],
            self.recv.at[18 + core * 4 + far],
            self.pos.holder(core, far),
        )

    def finish_step(self, step):
        size = 16 >> step
        for half in range(2):
            self.step_copy(half, step).wait()
            add_into(
                self.buf,
                (self.pos.core, half),
                self.from_step.at[half, pl.ds(32 - 2 * size, size)],
                self.base(half, step + 1),
                size,
            )
            if step == 0:
                self.step_copy(half, 1).start()
            else:
                for offset in range(1, 4):
                    self.axis_copy(half, offset).start()

    def stage(self, number):
        pos = self.pos
        if number == 0:
            self.core_copy().start()
        elif number == 1:
            self.core_copy().wait()
            for half in range(2):
                add_into(self.buf, (pos.core, half), self.from_core.at[half], 0, 32)
                self.step_copy(half, 0).start()
        elif number <= 3:
            self.finish_step(number - 2)
        elif number == 4:
            for half in range(2):
                for offset in range(1, 4):
                    self.axis_copy(half, offset).wait()
                own = self.buf[pos.core, half, pl.ds(self.axis_block(half, 0), 2)].astype(f32)
                for offset in range(3):
                    own = own + self.from_axis[half, offset].astype(f32)
                own = own.astype(bf16)
                for sub in range(2):
                    lanes = slice(sub * self.shift, sub * self.shift + self.window)
                    for near in range(2):
                        self.parts[(half * 2 + sub) * 2 + near] = own[near, :, lanes]
            for offset in range(1, 8):
                self.z_copy(offset).start()
        elif number == 5:
            for offset in range(1, 8):
                self.z_copy(offset).wait()
            total = self.parts[pos.z].astype(f32)
            for offset in range(7):
                total = total + self.from_z[offset].astype(f32)
            self.total[...] = total.astype(bf16)
            for offset in range(1, 8):
                self.delivery(offset).start()

            @pl.when(pos.own_rows())
            def _():
                self.own_delivery().start()

            @pl.when(jnp.logical_not(pos.own_rows()))
            def _():
                self.delivery(0).start()

        else:
            for offset in range(1, 8):
                self.delivery(offset).wait_send()

            @pl.when(pos.own_rows())
            def _():
                self.own_delivery().wait()

            @pl.when(jnp.logical_not(pos.own_rows()))
            def _():
                self.delivery(0).wait_send()

            for core in range(2):
                for far in range(4):
                    own = pos.own_rows() & (pos.core == core) & (pos.far == far)

                    @pl.when(jnp.logical_not(own))
                    def _():
                        self.arrival(core, far).wait_recv()


def block_index(core, half, space):
    z, x = space // 4, space % 4
    if half == 0:
        return ring_place[core][z // 2] * 8 + x * 2 + z % 2
    return ring_place[core][x] * 8 + z // 2 * 2 + z % 2


def kernel(
    feature,
    w1_hbm,
    wd_hbm,
    w2_hbm,
    upstream,
    rule1,
    rule2,
    child,
    send1,
    send2,
    count1,
    count2,
    coarse_out,
    input_grad,
    wide_out,
    thin_out,
    w1,
    wd,
    w2,
    table1,
    halo1,
    pack1,
    picked1,
    act1,
    pickedd,
    actd,
    coarse,
    pack2,
    halo2,
    picked2,
    back2,
    ext_grad2,
    give2,
    take2,
    grad_level,
    back1,
    ext_grad1,
    give1,
    take1,
    strips,
    wide_buf,
    wide_core,
    wide_step,
    wide_axis,
    wide_parts,
    wide_z,
    wide_total,
    wide_land,
    thin_buf,
    thin_core,
    thin_step,
    thin_axis,
    thin_parts,
    thin_z,
    thin_total,
    thin_land,
    load_sem,
    halo_send,
    halo_recv,
    wide_send,
    wide_recv,
    thin_send,
    thin_recv,
):
    pos = Position()
    greet(pos)
    wide_refs = (wide_buf, wide_core, wide_step, wide_axis, wide_parts, wide_z, wide_total, wide_land)
    thin_refs = (thin_buf, thin_core, thin_step, thin_axis, thin_parts, thin_z, thin_total, thin_land)
    wide = Reduction(pos, WINDOW, WIDE - WINDOW, wide_refs, wide_send, wide_recv)
    thin = Reduction(pos, THIN // 2, THIN // 2, thin_refs, thin_send, thin_recv)
    loads = [
        pltpu.make_async_copy(source, target, load_sem.at[i])
        for i, (source, target) in enumerate([(w1_hbm, w1), (wd_hbm, wd), (w2_hbm, w2)])
    ]
    for load in loads:
        load.start()

    def live_rows(rows, counts, width):
        lane = lax.broadcasted_iota(i32, (1, width), 1)
        return jnp.concatenate(
            [jnp.where(lane < counts[d], rows[d : d + 1, :], -1) for d in range(8)], axis=1
        )

    def exchange(number, source, target, sign):
        return [
            remote(
                source(d),
                target(d),
                halo_send.at[number, d],
                halo_recv.at[number, d],
                pos.brick(d, sign),
            )
            for d in range(8)
        ]

    def folded(d):
        return (pl.ds(d // 2 * C1, C1), pl.ds(d % 2 * H1, H1))

    def tap_rows(k, channels):
        return pl.ds(pl.multiple_of(k * channels, channels), channels)

    def fold(target, values):
        for w in range(4):
            target[w * C1 : (w + 1) * C1, :] = values[:, w * 256 : (w + 1) * 256]

    def unfold(values):
        return jnp.concatenate([values[w * C1 : (w + 1) * C1] for w in range(4)], axis=1)

    live1 = live_rows(send1, count1, H1)
    fold(table1, feature[...])
    pack1[...] = gather_four(table1[...], live1, 0)
    await_greetings(pos)
    copies = exchange(
        0, lambda d: pack1.at[:, pl.ds(d * H1, H1)], lambda d: halo1.at[folded(d)], 1
    )
    for copy in copies:
        copy.start()
    strips[...] = jnp.zeros_like(strips)
    picked2[TAPS * C2 :, :] = jnp.zeros((128, C2), bf16)

    def tap_one(k, _):
        picked1[tap_rows(k, C1), :] = gather_four(table1[...], rule1[k], 0)
        return 0

    lax.fori_loop(0, TAPS, tap_one, 0, unroll=9)
    for copy in copies:
        copy.wait()

    def tap_one_halo(k, _):
        here = (tap_rows(k, C1), slice(None))
        picked1[here] = picked1[here] + gather_four(halo1[...], rule1[k], V)
        return 0

    lax.fori_loop(0, TAPS, tap_one_halo, 0, unroll=9)
    loads[0].wait()
    act = dot(w1[...], picked1[...])
    act1[...] = act
    fold(table1, (feature[...].astype(f32) + silu(act)).astype(bf16))

    for m in range(8):
        pickedd[m * C1 : (m + 1) * C1, :] = gather_four(table1[...], child[m : m + 1, :], 0)
    loads[1].wait()
    act = dot(wd[...], pickedd[...])
    actd[...] = act
    coarse[...] = silu(act).astype(bf16)

    live2 = live_rows(send2, count2, H2)
    pack2[...] = dot(coarse[...], one_hot(live2, V2)).T.astype(bf16)
    copies = exchange(
        1, lambda d: pack2.at[pl.ds(d * H2, H2)], lambda d: halo2.at[pl.ds(d * H2, H2)], 1
    )
    for copy in copies:
        copy.start()

    def tap_two(k, _):
        picked2[tap_rows(k, C2), :] = dot(coarse[...], one_hot(rule2[k], V2)).astype(bf16)
        return 0

    lax.fori_loop(0, TAPS, tap_two, 0, unroll=9)
    for copy in copies:
        copy.wait()
    halo2[...] = halo2[...].astype(f32).T.astype(bf16)

    def tap_two_halo(k, _):
        here = (tap_rows(k, C2), slice(None))
        mine = dot(halo2[...], one_hot(rule2[k] - V2, V2)).astype(bf16)
        picked2[here] = picked2[here] + mine
        return 0

    lax.fori_loop(0, TAPS, tap_two_halo, 0, unroll=9)
    loads[2].wait()
    act = dot(w2[...], picked2[: TAPS * C2, :])
    coarse_out[...] = (coarse[...].astype(f32) + silu(act)).astype(bf16)
    grad_two = (upstream[...].astype(f32) * silu_grad(act)).astype(bf16)

    def spread_two(first):
        ext_grad2[...] = jnp.zeros_like(ext_grad2)

        def taps(t, _):
            total = ext_grad2[...]
            for j in range(9):
                k = t * 9 + j
                total += dot_nt(back2[tap_rows(k, C2), :], one_hot(rule2[k] - first, V2))
            ext_grad2[...] = total
            return 0

        lax.fori_loop(0, TAPS // 9, taps, 0)

    back2[...] = dot_tn(w2[...], grad_two).astype(bf16)
    spread_two(V2)
    give2[...] = ext_grad2[...].T.astype(bf16)
    copies = exchange(
        2, lambda d: give2.at[pl.ds(d * H2, H2)], lambda d: take2.at[pl.ds(d * H2, H2)], -1
    )
    for copy in copies:
        copy.start()
    for quarter in range(4):
        core, half = quarter // 2, quarter % 2
        upper = dot_nt(grad_two, picked2[quarter * WIDE : (quarter + 1) * WIDE, :])
        start = TAPS * V2 // 2 + quarter * WIDE
        lower = dot_nt(grad_two, picked2[start : start + WIDE, :])
        both = jnp.concatenate([upper.reshape(32, 8, WIDE), lower.reshape(32, 8, WIDE)], axis=1)
        both = both.astype(bf16)
        for space in range(32):
            wide_buf[core, half, block_index(core, half, space)] = both[space]
    wide.stage(0)
    spread_two(0)
    wide.stage(1)
    for copy in copies:
        copy.wait()
    returned = dot(one_hot(live2, V2), take2[...]).T
    grad_coarse = upstream[...].astype(f32) + ext_grad2[...] + returned
    grad_down = (grad_coarse * silu_grad(actd[...])).astype(bf16)

    backd = dot_tn(wd[...], grad_down).astype(bf16)
    total = jnp.zeros((4 * C1, 256), f32)
    for m in range(8):
        total += scatter_four(backd[m * C1 : (m + 1) * C1], child[m : m + 1, :], 0)
    grad_level[...] = total
    wide.stage(2)
    grad_one = (unfold(total) * silu_grad(act1[...])).astype(bf16)
    term_down = dot_nt(grad_down, pickedd[...]).reshape(32, 8, 768)
    term_one = dot_nt(grad_one, picked1[...]).astype(bf16)
    for q in range(5):
        width = min(640, TAPS * C1 - q * 640)
        strips[q * C1 : (q + 1) * C1, :width] = term_one[:, q * 640 : q * 640 + width]
    spot = lax.broadcasted_iota(i32, (1, 5 * C1), 1)
    strip, out_row = spot // C1, spot % C1
    spot = (out_row // 3) * 16 + (out_row % 3) * 5 + strip
    first = dot(one_hot(spot, 512), strips[...]).reshape(32, 16, 640)
    other = jnp.concatenate([term_down[:, :, :384], term_down[:, :, 384:]], axis=1)
    for quarter in range(4):
        core, half = quarter // 2, quarter % 2
        low, high = quarter * THIN, (quarter + 1) * THIN
        if high <= 640:
            both = first[:, :, low:high]
        elif low >= 640:
            both = other[:, :, low - 640 : high - 640]
        else:
            both = jnp.concatenate([first[:, :, low:], other[:, :, : high - 640]], axis=2)
        both = both.astype(bf16)
        for space in range(32):
            thin_buf[core, half, block_index(core, half, space)] = both[space]
    thin.stage(0)
    wide.stage(3)

    back1[...] = dot_tn(w1[...], grad_one).astype(bf16)

    def spread_one(first, beside):
        ext_grad1[...] = jnp.zeros_like(ext_grad1)

        def taps(t, _):
            for when, stages in beside.items():

                @pl.when(t == when)
                def _():
                    for reduction, number in stages:
                        reduction.stage(number)

            total = ext_grad1[...]
            for j in range(9):
                k = t * 9 + j
                total += scatter_four(back1[tap_rows(k, C1), :], rule1[k], first)
            ext_grad1[...] = total
            return 0

        lax.fori_loop(0, TAPS // 9, taps, 0)

    spread_one(V, {1: [(thin, 1)], 2: [(wide, 4), (thin, 2)]})
    give1[...] = ext_grad1[...].astype(bf16)
    copies = exchange(
        3, lambda d: give1.at[folded(d)], lambda d: take1.at[:, pl.ds(d * H1, H1)], -1
    )
    for copy in copies:
        copy.start()
    thin.stage(3)
    spread_one(0, {1: [(thin, 4), (wide, 5)], 2: [(thin, 5)]})
    for copy in copies:
        copy.wait()
    total = grad_level[...] + ext_grad1[...] + scatter_four(take1[...], live1, 0)
    input_grad[...] = unfold(total).astype(bf16)
    thin.stage(6)
    wide.stage(6)
    thin_out[...] = thin_land[...]
    wide_out[...] = wide_land[...]


def finish(coarse_in, input_in, wide_in, thin_in, coarse_out, input_grad, gw1, gwd, gw2):
    coarse_out[...] = coarse_in[...]
    input_grad[...] = input_in[...]
    scale = 1.0 / 256
    for quarter in range(4):
        core, half = quarter // 2, quarter % 2
        low, high = wide_in[core, half * 2], wide_in[core, half * 2 + 1]
        piece = jnp.concatenate([low, high[:, 2 * WINDOW - WIDE :]], axis=1).astype(f32) * scale
        for side in range(2):
            start = quarter * WIDE
            width = min(WIDE, TAPS * V2 // 2 - start)
            here = side * TAPS * V2 // 2 + start
            gw2[:, here : here + width] = piece[side * 8 : side * 8 + 8, :width]
    pieces = [thin_in[q // 4, q % 4].astype(f32) * scale for q in range(8)]
    thin_all = jnp.concatenate(pieces, axis=1)
    gwd[:, :384] = thin_all[:8, 640:]
    gwd[:, 384:] = thin_all[8:, 640:]
    for r in range(3):
        for q in range(5):
            width = min(640, TAPS * C1 - q * 640)
            row = r * 5 + q
            gw1[r : r + 1, q * 640 : q * 640 + width] = thin_all[row : row + 1, :width]


def reduction_scratch(lanes, window):
    return [
        pltpu.VMEM((2, 2, 32, 16, lanes), bf16),
        pltpu.VMEM((2, 32, 16, lanes), bf16),
        pltpu.VMEM((2, 24, 16, lanes), bf16),
        pltpu.VMEM((2, 3, 2, 16, lanes), bf16),
        pltpu.VMEM((8, 16, window), bf16),
        pltpu.VMEM((7, 16, window), bf16),
        pltpu.VMEM((16, window), bf16),
        pltpu.VMEM((2, 4, 16, window), bf16),
    ]


def run_kernels(*operands):
    vmem = pl.BlockSpec(memory_space=pltpu.VMEM)
    smem = pl.BlockSpec(memory_space=pltpu.SMEM)
    away = pl.BlockSpec(memory_space=pl.ANY)
    dma = pltpu.SemaphoreType.DMA
    results = pl.pallas_call(
        kernel,
        out_shape=(
            jax.ShapeDtypeStruct((C2, V2), bf16),
            jax.ShapeDtypeStruct((C1, V), bf16),
            jax.ShapeDtypeStruct((2, 4, 16, WINDOW), bf16),
            jax.ShapeDtypeStruct((2, 4, 16, THIN // 2), bf16),
        ),
        in_specs=[vmem] + [away] * 3 + [vmem] * 6 + [smem] * 2,
        out_specs=[vmem] * 4,
        scratch_shapes=[
            pltpu.VMEM((C1, TAPS * C1), bf16),
            pltpu.VMEM((C2, 8 * C1), bf16),
            pltpu.VMEM((C2, TAPS * C2), bf16),
            pltpu.VMEM((4 * C1, 256), bf16),
            pltpu.VMEM((4 * C1, 256), bf16),
            pltpu.VMEM((C1, V), bf16),
            pltpu.VMEM((TAPS * C1, V), bf16),
            pltpu.VMEM((C1, V), f32),
            pltpu.VMEM((8 * C1, V2), bf16),
            pltpu.VMEM((C2, V2), f32),
            pltpu.VMEM((C2, V2), bf16),
            pltpu.VMEM((V2, C2), bf16),
            pltpu.VMEM((V2, C2), bf16),
            pltpu.VMEM((TAPS * C2 + 128, V2), bf16),
            pltpu.VMEM((TAPS * C2, V2), bf16),
            pltpu.VMEM((C2, V2), f32),
            pltpu.VMEM((V2, C2), bf16),
            pltpu.VMEM((V2, C2), bf16),
            pltpu.VMEM((4 * C1, 256), f32),
            pltpu.VMEM((TAPS * C1, V), bf16),
            pltpu.VMEM((4 * C1, 256), f32),
            pltpu.VMEM((4 * C1, 256), bf16),
            pltpu.VMEM((C1, V), bf16),
            pltpu.VMEM((5 * C1, 640), bf16),
            *reduction_scratch(WIDE, WINDOW),
            *reduction_scratch(THIN, THIN // 2),
            dma((3,)),
            dma((4, 8)),
            dma((4, 8)),
            dma((26,)),
            dma((26,)),
            dma((26,)),
            dma((26,)),
        ],
        compiler_params=pltpu.CompilerParams(
            collective_id=0, has_side_effects=True, vmem_limit_bytes=58 << 20
        ),
    )(*operands)
    return pl.pallas_call(
        finish,
        out_shape=(
            jax.ShapeDtypeStruct((C2, V2), bf16),
            jax.ShapeDtypeStruct((C1, V), bf16),
            jax.ShapeDtypeStruct((3, TAPS * C1), f32),
            jax.ShapeDtypeStruct((8, 8 * C1), f32),
            jax.ShapeDtypeStruct((8, TAPS * C2), f32),
        ),
        in_specs=[vmem] * 4,
        out_specs=[vmem] * 5,
    )(*results)


def body(
    features,
    weight_one,
    weight_down,
    weight_two,
    cotangent,
    rule_one,
    rule_two,
    children,
    send_one,
    count_one,
    send_two,
    count_two,
):
    coarse_out, input_grad, gw1, gwd, gw2 = run_kernels(
        features[0],
        weight_one,
        weight_down,
        weight_two,
        cotangent[0],
        rule_one.transpose(1, 0, 2),
        rule_two.transpose(1, 0, 2),
        children[0],
        send_one[0, 0],
        send_two[0, 0],
        count_one[0, 0],
        count_two[0, 0],
    )
    return coarse_out[None], input_grad[None], gw1, gwd, gw2


def solution(mesh):
    tile = P("dp", None, "space")
    brick = P("dp", "space", None, None)
    count = P("dp", "space", None)
    return jax.shard_map(
        body,
        mesh=mesh,
        in_specs=(tile, P(), P(), P(), tile, tile, tile, tile, brick, count, brick, count),
        out_specs=(tile, tile, P("space", None), P("space", None), P("space", None)),
        check_vma=False,
    )
```

```python
import jax
import jax.numpy as jnp
from jax import lax
from jax.experimental import pallas as pl
from jax.experimental.pallas import tpu as pltpu
from jax.sharding import PartitionSpec as P

bf16 = jnp.bfloat16
f32 = jnp.float32
i32 = jnp.int32
C1, C2, V, V2, H1, H2, TAPS = 96, 256, 1024, 256, 128, 32, 27
WIDE = 896
WIDE_PIECE, THIN_PIECE = 256, 128
directions = ((-1, -1), (-1, 0), (-1, 1), (0, -1), (0, 1), (1, -1), (1, 0), (1, 1))
ring_place = ((0, 2, 3, 1), (0, 1, 3, 2))


def dot(a, b):
    return jnp.dot(a, b, preferred_element_type=f32)


def dot_nt(a, b):
    return lax.dot_general(a, b, (((1,), (1,)), ((), ())), preferred_element_type=f32)


def dot_tn(a, b):
    return lax.dot_general(a, b, (((0,), (0,)), ((), ())), preferred_element_type=f32)


def one_hot(row, size):
    return jnp.where(
        lax.broadcasted_iota(jnp.int16, (size, row.shape[1]), 0) == row.astype(jnp.int16),
        jnp.ones((), bf16),
        jnp.zeros((), bf16),
    )


def logistic(v):
    return 1.0 / (1.0 + jnp.exp(-v))


def silu(v):
    return v * logistic(v)


def silu_grad(v):
    s = logistic(v)
    return s * (1.0 + v * (1.0 - s))


def place():
    return lax.axis_index("dp"), lax.axis_index("space")


def remote(src, dst, send_sem, recv_sem, device):
    return pltpu.make_async_remote_copy(
        src_ref=src,
        dst_ref=dst,
        send_sem=send_sem,
        recv_sem=recv_sem,
        device_id=device,
        device_id_type=pl.DeviceIdType.MESH,
    )


def greet(devices):
    barrier = pltpu.get_barrier_semaphore()
    for device in devices:
        pl.semaphore_signal(barrier, inc=1, device_id=device, device_id_type=pl.DeviceIdType.MESH)


def await_greetings(devices):
    pl.semaphore_wait(pltpu.get_barrier_semaphore(), len(devices))


def in_table(row, first):
    return jnp.where((row >= first) & (row < first + V), row & 255, -1)


def gather_four(table, row, first):
    both = dot(table, one_hot(in_table(row, first), 256))
    odd, upper = (row & 256) != 0, (row & 512) != 0
    low = jnp.where(odd, both[C1 : 2 * C1], both[:C1])
    high = jnp.where(odd, both[3 * C1 :], both[2 * C1 : 3 * C1])
    return jnp.where(upper, high, low).astype(bf16)


def scatter_four(values, row, first):
    place_four = (row >> 8) & 3
    zero = jnp.zeros_like(values)
    spread = jnp.concatenate(
        [jnp.where(place_four == w, values, zero) for w in range(4)], axis=0
    )
    return dot_nt(spread, one_hot(in_table(row, first), 256))


class Position:
    def __init__(self):
        self.dp, self.space = place()
        self.y, self.core = self.dp // 2, self.dp % 2
        self.z, self.x = self.space // 4, self.space % 4

    def brick(self, direction, sign):
        dy, dx = directions[direction]
        gy = (self.space // 8 + sign * dy + 4) % 4
        gx = (self.space % 8 + sign * dx + 8) % 8
        return (self.dp, gy * 8 + gx)

    def other_core(self):
        return (self.y * 2 + 1 - self.core, self.space)

    def at_y(self, y):
        return (y * 2 + self.core, self.space)

    def at_x(self, x):
        return (self.dp, self.z * 4 + x)

    def at_z(self, z):
        return (self.dp, z * 4 + self.x)

    def gray(self, v):
        return (v + v // 2) % 2

    def flip(self, v):
        return v + 1 - 2 * (v % 2)

    def halving(self, axis, step):
        v, at = (self.y, self.at_y) if axis == "y" else (self.x, self.at_x)
        first = 1 - self.core if step == 0 else self.core
        keep = first * self.gray(v) + (1 - first) * (v // 2)
        return keep, at(first * self.flip(v) + (1 - first) * (3 - v))

    def at_axis(self, axis, offset):
        if axis == "y":
            return self.at_y((self.y + offset) % 4)
        return self.at_x((self.x + offset) % 4)

    def in_row(self, offset):
        return ((self.dp + offset) % 8, self.space)

    def partners(self):
        return (
            [self.brick(d, 1) for d in range(8)]
            + [self.in_row(offset) for offset in range(1, 8)]
            + [self.at_axis("x", offset) for offset in range(1, 4)]
            + [self.at_z((self.z + offset) % 8) for offset in (1, 3, 4, 5, 7)]
        )


def add_into(target, index, source, start, count):
    def part(i, _):
        here = index + (pl.ds(start + i * 16, 16),)
        total = target[here].astype(f32) + source[pl.ds(i * 16, 16)].astype(f32)
        target[here] = total.astype(bf16)
        return 0

    lax.fori_loop(0, count // 16, part, 0)


def block_index(core, axes, piece, space):
    z, x = space // 4, space % 4
    first, second = (piece, x) if axes == "yx" else (x, piece)
    return ring_place[core][first] * 32 + second * 8 + z


class Reduction:
    def __init__(self, pos, axes, refs, send, recv):
        self.pos, self.axes = pos, axes
        self.buf, self.from_core, self.from_step, self.from_axis = refs[:4]
        self.parts, self.from_z, self.total, self.landed = refs[4:]
        self.send, self.recv = send, recv

    def copy(self, source, target, sem, device):
        return remote(source, target, self.send.at[sem], self.recv.at[sem], device)

    def core_copy(self):
        pos = self.pos
        return self.copy(self.buf.at[1 - pos.core], self.from_core, 0, pos.other_core())

    def base(self, half, steps):
        start, size = 0, 128
        for step in range(steps):
            size //= 2
            start = start + self.pos.halving(self.axes[half][0], step)[0] * size
        return start

    def step_copy(self, half, step):
        size = 64 >> step
        keep, partner = self.pos.halving(self.axes[half][0], step)
        start = self.base(half, step) + (1 - keep) * size
        return self.copy(
            self.buf.at[self.pos.core, half, pl.ds(start, size)],
            self.from_step.at[half, pl.ds(128 - 2 * size, size)],
            1 + half * 2 + step,
            partner,
        )

    def axis_block(self, half, offset):
        v = self.pos.x if self.axes[half] == "yx" else self.pos.y
        return self.base(half, 2) + (v + offset) % 4 * 8

    def axis_copy(self, half, offset):
        return self.copy(
            self.buf.at[self.pos.core, half, pl.ds(self.axis_block(half, offset), 8)],
            self.from_axis.at[half, offset - 1],
            4 + half * 3 + offset,
            self.pos.at_axis(self.axes[half][1], offset),
        )

    def z_copy(self, offset):
        z = (self.pos.z + offset) % 8
        return self.copy(
            self.parts.at[z], self.from_z.at[offset - 1], 10 + offset, self.pos.at_z(z)
        )

    def delivery(self, offset):
        return self.copy(
            self.total, self.landed.at[offset], 17 + offset, self.pos.in_row(offset)
        )

    def stage(self, number):
        pos = self.pos
        halves = range(len(self.axes))
        if number == 0:
            self.core_copy().start()
        elif number == 1:
            self.core_copy().wait()
            for half in halves:
                add_into(self.buf, (pos.core, half), self.from_core.at[half], 0, 128)
                self.step_copy(half, 0).start()
        elif number <= 3:
            size = 64 >> (number - 2)
            for half in halves:
                self.step_copy(half, number - 2).wait()
                add_into(
                    self.buf,
                    (pos.core, half),
                    self.from_step.at[half, pl.ds(128 - 2 * size, size)],
                    self.base(half, number - 1),
                    size,
                )
                if number == 2:
                    self.step_copy(half, 1).start()
                else:
                    for offset in range(1, 4):
                        self.axis_copy(half, offset).start()
        elif number == 4:
            for half in halves:
                for offset in range(1, 4):
                    self.axis_copy(half, offset).wait()
                own = self.buf[pos.core, half, pl.ds(self.axis_block(half, 0), 8)].astype(f32)
                for offset in range(3):
                    own = own + self.from_axis[half, offset].astype(f32)
                self.parts[:, half] = own.astype(bf16)
            for offset in range(1, 8):
                self.z_copy(offset).start()
        elif number == 5:
            for offset in range(1, 8):
                self.z_copy(offset).wait()
            total = self.parts[pos.z].astype(f32)
            for offset in range(7):
                total = total + self.from_z[offset].astype(f32)
            self.total[...] = total.astype(bf16)
            for offset in range(1, 8):
                self.delivery(offset).start()
        else:
            for offset in range(1, 8):
                self.delivery(offset).wait()
            self.landed[0] = self.total[...]

    def result(self, core, piece):
        return self.landed[(self.pos.dp - (piece * 2 + core) + 8) % 8]


def kernel(
    feature,
    w1_hbm,
    wd_hbm,
    w2_hbm,
    upstream,
    rule1,
    rule2,
    child,
    send1,
    send2,
    count1,
    count2,
    coarse_out,
    input_grad,
    wide_out,
    thin_out,
    w1,
    wd,
    w2,
    table1,
    halo1,
    pack1,
    picked1,
    act1,
    pickedd,
    actd,
    coarse,
    pack2,
    halo2,
    picked2,
    back2,
    ext_grad2,
    give2,
    take2,
    grad_level,
    back1,
    ext_grad1,
    give1,
    take1,
    strips,
    wide_buf,
    wide_core,
    wide_step,
    wide_axis,
    wide_parts,
    wide_z,
    wide_total,
    wide_land,
    thin_buf,
    thin_core,
    thin_step,
    thin_axis,
    thin_parts,
    thin_z,
    thin_total,
    thin_land,
    load_sem,
    halo_send,
    halo_recv,
    wide_send,
    wide_recv,
    thin_send,
    thin_recv,
):
    pos = Position()
    greet(pos.partners())
    wide_refs = (wide_buf, wide_core, wide_step, wide_axis, wide_parts, wide_z, wide_total, wide_land)
    thin_refs = (thin_buf, thin_core, thin_step, thin_axis, thin_parts, thin_z, thin_total, thin_land)
    wide = Reduction(pos, ("yx", "xy"), wide_refs, wide_send, wide_recv)
    thin = Reduction(pos, ("yx",), thin_refs, thin_send, thin_recv)
    loads = [
        pltpu.make_async_copy(source, target, load_sem.at[i])
        for i, (source, target) in enumerate([(w1_hbm, w1), (wd_hbm, wd), (w2_hbm, w2)])
    ]
    for load in loads:
        load.start()

    def live_rows(rows, counts, width):
        lane = lax.broadcasted_iota(i32, (1, width), 1)
        return jnp.concatenate(
            [jnp.where(lane < counts[d], rows[d : d + 1, :], -1) for d in range(8)], axis=1
        )

    def exchange(number, source, target, sign):
        return [
            remote(
                source(d),
                target(d),
                halo_send.at[number, d],
                halo_recv.at[number, d],
                pos.brick(d, sign),
            )
            for d in range(8)
        ]

    def folded(d):
        return (pl.ds(d // 2 * C1, C1), pl.ds(d % 2 * H1, H1))

    def tap_rows(k, channels):
        return pl.ds(pl.multiple_of(k * channels, channels), channels)

    def fold(target, values):
        for w in range(4):
            target[w * C1 : (w + 1) * C1, :] = values[:, w * 256 : (w + 1) * 256]

    def unfold(values):
        return jnp.concatenate([values[w * C1 : (w + 1) * C1] for w in range(4)], axis=1)

    live1 = live_rows(send1, count1, H1)
    fold(table1, feature[...])
    pack1[...] = gather_four(table1[...], live1, 0)
    await_greetings(pos.partners())
    copies = exchange(
        0, lambda d: pack1.at[:, pl.ds(d * H1, H1)], lambda d: halo1.at[folded(d)], 1
    )
    for copy in copies:
        copy.start()
    strips[...] = jnp.zeros_like(strips)
    picked2[TAPS * C2 :, :] = jnp.zeros((128, C2), bf16)

    def tap_one(k, _):
        picked1[tap_rows(k, C1), :] = gather_four(table1[...], rule1[k], 0)
        return 0

    lax.fori_loop(0, TAPS, tap_one, 0, unroll=9)
    for copy in copies:
        copy.wait()

    def tap_one_halo(k, _):
        here = (tap_rows(k, C1), slice(None))
        picked1[here] = picked1[here] + gather_four(halo1[...], rule1[k], V)
        return 0

    lax.fori_loop(0, TAPS, tap_one_halo, 0, unroll=9)
    loads[0].wait()
    act = dot(w1[...], picked1[...])
    act1[...] = act
    fold(table1, (feature[...].astype(f32) + silu(act)).astype(bf16))

    for m in range(8):
        pickedd[m * C1 : (m + 1) * C1, :] = gather_four(table1[...], child[m : m + 1, :], 0)
    loads[1].wait()
    act = dot(wd[...], pickedd[...])
    actd[...] = act
    coarse[...] = silu(act).astype(bf16)

    live2 = live_rows(send2, count2, H2)
    pack2[...] = dot(coarse[...], one_hot(live2, V2)).T.astype(bf16)
    copies = exchange(
        1, lambda d: pack2.at[pl.ds(d * H2, H2)], lambda d: halo2.at[pl.ds(d * H2, H2)], 1
    )
    for copy in copies:
        copy.start()

    def tap_two(k, _):
        picked2[tap_rows(k, C2), :] = dot(coarse[...], one_hot(rule2[k], V2)).astype(bf16)
        return 0

    lax.fori_loop(0, TAPS, tap_two, 0, unroll=9)
    for copy in copies:
        copy.wait()
    halo2[...] = halo2[...].astype(f32).T.astype(bf16)

    def tap_two_halo(k, _):
        here = (tap_rows(k, C2), slice(None))
        mine = dot(halo2[...], one_hot(rule2[k] - V2, V2)).astype(bf16)
        picked2[here] = picked2[here] + mine
        return 0

    lax.fori_loop(0, TAPS, tap_two_halo, 0, unroll=9)
    loads[2].wait()
    act = dot(w2[...], picked2[: TAPS * C2, :])
    coarse_out[...] = (coarse[...].astype(f32) + silu(act)).astype(bf16)
    grad_two = (upstream[...].astype(f32) * silu_grad(act)).astype(bf16)

    def spread_two(first):
        ext_grad2[...] = jnp.zeros_like(ext_grad2)

        def taps(t, _):
            total = ext_grad2[...]
            for j in range(9):
                k = t * 9 + j
                total += dot_nt(back2[tap_rows(k, C2), :], one_hot(rule2[k] - first, V2))
            ext_grad2[...] = total
            return 0

        lax.fori_loop(0, TAPS // 9, taps, 0)

    back2[...] = dot_tn(w2[...], grad_two).astype(bf16)
    spread_two(V2)
    give2[...] = ext_grad2[...].T.astype(bf16)
    copies = exchange(
        2, lambda d: give2.at[pl.ds(d * H2, H2)], lambda d: take2.at[pl.ds(d * H2, H2)], -1
    )
    for copy in copies:
        copy.start()
    for quarter in range(4):
        core, half = quarter // 2, quarter % 2
        upper = dot_nt(grad_two, picked2[quarter * WIDE : (quarter + 1) * WIDE, :])
        start = TAPS * V2 // 2 + quarter * WIDE
        lower = dot_nt(grad_two, picked2[start : start + WIDE, :])
        both = jnp.concatenate([upper.reshape(32, 8, WIDE), lower.reshape(32, 8, WIDE)], axis=1)
        both = both.astype(bf16)
        for piece in range(4):
            low = min(piece * WIDE_PIECE, WIDE - WIDE_PIECE)
            for space in range(32):
                block = block_index(core, wide.axes[half], piece, space)
                wide_buf[core, half, block] = both[space][:, low : low + WIDE_PIECE]
    wide.stage(0)
    spread_two(0)
    wide.stage(1)
    for copy in copies:
        copy.wait()
    returned = dot(one_hot(live2, V2), take2[...]).T
    grad_coarse = upstream[...].astype(f32) + ext_grad2[...] + returned
    grad_down = (grad_coarse * silu_grad(actd[...])).astype(bf16)

    backd = dot_tn(wd[...], grad_down).astype(bf16)
    total = jnp.zeros((4 * C1, 256), f32)
    for m in range(8):
        total += scatter_four(backd[m * C1 : (m + 1) * C1], child[m : m + 1, :], 0)
    grad_level[...] = total
    wide.stage(2)
    grad_one = (unfold(total) * silu_grad(act1[...])).astype(bf16)
    term_down = dot_nt(grad_down, pickedd[...]).reshape(32, 8, 768)
    term_one = dot_nt(grad_one, picked1[...]).astype(bf16)
    for q in range(5):
        width = min(640, TAPS * C1 - q * 640)
        strips[q * C1 : (q + 1) * C1, :width] = term_one[:, q * 640 : q * 640 + width]
    spot = lax.broadcasted_iota(i32, (1, 5 * C1), 1)
    strip, out_row = spot // C1, spot % C1
    spot = (out_row // 3) * 16 + (out_row % 3) * 5 + strip
    first = dot(one_hot(spot, 512), strips[...]).reshape(32, 16, 640)
    other = jnp.concatenate([term_down[:, :, :384], term_down[:, :, 384:]], axis=1)
    for tile in range(8):
        core, piece = tile // 4, tile % 4
        both = first if tile < 5 else other
        low = tile % 5 * THIN_PIECE
        both = both[:, :, low : low + THIN_PIECE].astype(bf16)
        for space in range(32):
            thin_buf[core, 0, block_index(core, thin.axes[0], piece, space)] = both[space]
    thin.stage(0)
    wide.stage(3)

    back1[...] = dot_tn(w1[...], grad_one).astype(bf16)

    def spread_one(first, beside):
        ext_grad1[...] = jnp.zeros_like(ext_grad1)

        def taps(t, _):
            for when, stages in beside.items():

                @pl.when(t == when)
                def _():
                    for reduction, number in stages:
                        reduction.stage(number)

            total = ext_grad1[...]
            for j in range(9):
                k = t * 9 + j
                total += scatter_four(back1[tap_rows(k, C1), :], rule1[k], first)
            ext_grad1[...] = total
            return 0

        lax.fori_loop(0, TAPS // 9, taps, 0)

    spread_one(V, {1: [(thin, 1)], 2: [(wide, 4), (thin, 2)]})
    give1[...] = ext_grad1[...].astype(bf16)
    copies = exchange(
        3, lambda d: give1.at[folded(d)], lambda d: take1.at[:, pl.ds(d * H1, H1)], -1
    )
    for copy in copies:
        copy.start()
    thin.stage(3)
    spread_one(0, {1: [(thin, 4), (wide, 5)], 2: [(thin, 5)]})
    for copy in copies:
        copy.wait()
    total = grad_level[...] + ext_grad1[...] + scatter_four(take1[...], live1, 0)
    input_grad[...] = unfold(total).astype(bf16)
    thin.stage(6)
    wide.stage(6)
    for core in range(2):
        for piece in range(4):
            thin_out[core, piece] = thin.result(core, piece)
            wide_out[core, piece] = wide.result(core, piece)


def finish(coarse_in, input_in, wide_in, thin_in, coarse_out, input_grad, gw1, gwd, gw2):
    coarse_out[...] = coarse_in[...]
    input_grad[...] = input_in[...]
    scale = 1.0 / 256
    for quarter in range(4):
        core, half = quarter // 2, quarter % 2
        piece = [wide_in[core, j, half] for j in range(4)]
        piece[3] = piece[3][:, 4 * WIDE_PIECE - WIDE :]
        piece = jnp.concatenate(piece, axis=1).astype(f32) * scale
        for side in range(2):
            start = quarter * WIDE
            width = min(WIDE, TAPS * V2 // 2 - start)
            here = side * TAPS * V2 // 2 + start
            gw2[:, here : here + width] = piece[side * 8 : side * 8 + 8, :width]
    pieces = [thin_in[q // 4, q % 4, 0].astype(f32) * scale for q in range(8)]
    thin_all = jnp.concatenate(pieces, axis=1)
    gwd[:, :384] = thin_all[:8, 640:]
    gwd[:, 384:] = thin_all[8:, 640:]
    for r in range(3):
        for q in range(5):
            width = min(640, TAPS * C1 - q * 640)
            row = r * 5 + q
            gw1[r : r + 1, q * 640 : q * 640 + width] = thin_all[row : row + 1, :width]


def reduction_scratch(halves, lanes):
    return [
        pltpu.VMEM((2, halves, 128, 16, lanes), bf16),
        pltpu.VMEM((halves, 128, 16, lanes), bf16),
        pltpu.VMEM((halves, 96, 16, lanes), bf16),
        pltpu.VMEM((halves, 3, 8, 16, lanes), bf16),
        pltpu.VMEM((8, halves, 16, lanes), bf16),
        pltpu.VMEM((7, halves, 16, lanes), bf16),
        pltpu.VMEM((halves, 16, lanes), bf16),
        pltpu.VMEM((8, halves, 16, lanes), bf16),
    ]


def run_kernels(*operands):
    vmem = pl.BlockSpec(memory_space=pltpu.VMEM)
    smem = pl.BlockSpec(memory_space=pltpu.SMEM)
    away = pl.BlockSpec(memory_space=pl.ANY)
    dma = pltpu.SemaphoreType.DMA
    results = pl.pallas_call(
        kernel,
        out_shape=(
            jax.ShapeDtypeStruct((C2, V2), bf16),
            jax.ShapeDtypeStruct((C1, V), bf16),
            jax.ShapeDtypeStruct((2, 4, 2, 16, WIDE_PIECE), bf16),
            jax.ShapeDtypeStruct((2, 4, 1, 16, THIN_PIECE), bf16),
        ),
        in_specs=[vmem] + [away] * 3 + [vmem] * 6 + [smem] * 2,
        out_specs=[vmem] * 4,
        scratch_shapes=[
            pltpu.VMEM((C1, TAPS * C1), bf16),
            pltpu.VMEM((C2, 8 * C1), bf16),
            pltpu.VMEM((C2, TAPS * C2), bf16),
            pltpu.VMEM((4 * C1, 256), bf16),
            pltpu.VMEM((4 * C1, 256), bf16),
            pltpu.VMEM((C1, V), bf16),
            pltpu.VMEM((TAPS * C1, V), bf16),
            pltpu.VMEM((C1, V), f32),
            pltpu.VMEM((8 * C1, V2), bf16),
            pltpu.VMEM((C2, V2), f32),
            pltpu.VMEM((C2, V2), bf16),
            pltpu.VMEM((V2, C2), bf16),
            pltpu.VMEM((V2, C2), bf16),
            pltpu.VMEM((TAPS * C2 + 128, V2), bf16),
            pltpu.VMEM((TAPS * C2, V2), bf16),
            pltpu.VMEM((C2, V2), f32),
            pltpu.VMEM((V2, C2), bf16),
            pltpu.VMEM((V2, C2), bf16),
            pltpu.VMEM((4 * C1, 256), f32),
            pltpu.VMEM((TAPS * C1, V), bf16),
            pltpu.VMEM((4 * C1, 256), f32),
            pltpu.VMEM((4 * C1, 256), bf16),
            pltpu.VMEM((C1, V), bf16),
            pltpu.VMEM((5 * C1, 640), bf16),
            *reduction_scratch(2, WIDE_PIECE),
            *reduction_scratch(1, THIN_PIECE),
            dma((3,)),
            dma((4, 8)),
            dma((4, 8)),
            dma((26,)),
            dma((26,)),
            dma((26,)),
            dma((26,)),
        ],
        compiler_params=pltpu.CompilerParams(
            collective_id=0, has_side_effects=True, vmem_limit_bytes=58 << 20
        ),
    )(*operands)
    return pl.pallas_call(
        finish,
        out_shape=(
            jax.ShapeDtypeStruct((C2, V2), bf16),
            jax.ShapeDtypeStruct((C1, V), bf16),
            jax.ShapeDtypeStruct((3, TAPS * C1), f32),
            jax.ShapeDtypeStruct((8, 8 * C1), f32),
            jax.ShapeDtypeStruct((8, TAPS * C2), f32),
        ),
        in_specs=[vmem] * 4,
        out_specs=[vmem] * 5,
    )(*results)


def body(
    features,
    weight_one,
    weight_down,
    weight_two,
    cotangent,
    rule_one,
    rule_two,
    children,
    send_one,
    count_one,
    send_two,
    count_two,
):
    coarse_out, input_grad, gw1, gwd, gw2 = run_kernels(
        features[0],
        weight_one,
        weight_down,
        weight_two,
        cotangent[0],
        rule_one.transpose(1, 0, 2),
        rule_two.transpose(1, 0, 2),
        children[0],
        send_one[0, 0],
        send_two[0, 0],
        count_one[0, 0],
        count_two[0, 0],
    )
    return coarse_out[None], input_grad[None], gw1, gwd, gw2


def solution(mesh):
    tile = P("dp", None, "space")
    brick = P("dp", "space", None, None)
    count = P("dp", "space", None)
    return jax.shard_map(
        body,
        mesh=mesh,
        in_specs=(tile, P(), P(), P(), tile, tile, tile, tile, brick, count, brick, count),
        out_specs=(tile, tile, P("space", None), P("space", None), P("space", None)),
        check_vma=False,
    )
```

```python
import jax
import jax.numpy as jnp
from jax import lax
from jax.experimental import pallas as pl
from jax.experimental.pallas import tpu as pltpu
from jax.sharding import PartitionSpec as P

bf16 = jnp.bfloat16
f32 = jnp.float32
i32 = jnp.int32
C1, C2, V, V2, H1, H2, TAPS = 96, 256, 1024, 256, 128, 32, 27
WIDE = 896
WIDE_PIECE, THIN_PIECE = 256, 128
directions = ((-1, -1), (-1, 0), (-1, 1), (0, -1), (0, 1), (1, -1), (1, 0), (1, 1))
ring_place = ((0, 2, 3, 1), (0, 1, 3, 2))


def dot(a, b):
    return jnp.dot(a, b, preferred_element_type=f32)


def dot_nt(a, b):
    return lax.dot_general(a, b, (((1,), (1,)), ((), ())), preferred_element_type=f32)


def dot_tn(a, b):
    return lax.dot_general(a, b, (((0,), (0,)), ((), ())), preferred_element_type=f32)


def one_hot(row, size):
    return jnp.where(
        lax.broadcasted_iota(jnp.int16, (size, row.shape[1]), 0) == row.astype(jnp.int16),
        jnp.ones((), bf16),
        jnp.zeros((), bf16),
    )


def logistic(v):
    return 1.0 / (1.0 + jnp.exp(-v))


def silu(v):
    return v * logistic(v)


def silu_grad(v):
    s = logistic(v)
    return s * (1.0 + v * (1.0 - s))


def place():
    return lax.axis_index("dp"), lax.axis_index("space")


def remote(src, dst, send_sem, recv_sem, device):
    return pltpu.make_async_remote_copy(
        src_ref=src,
        dst_ref=dst,
        send_sem=send_sem,
        recv_sem=recv_sem,
        device_id=device,
        device_id_type=pl.DeviceIdType.MESH,
    )


def greet(devices):
    barrier = pltpu.get_barrier_semaphore()
    for device in devices:
        pl.semaphore_signal(barrier, inc=1, device_id=device, device_id_type=pl.DeviceIdType.MESH)


def await_greetings(devices):
    pl.semaphore_wait(pltpu.get_barrier_semaphore(), len(devices))


def in_table(row, first):
    return jnp.where((row >= first) & (row < first + V), row & 255, -1)


def gather_four(table, row, first):
    both = dot(table, one_hot(in_table(row, first), 256))
    odd, upper = (row & 256) != 0, (row & 512) != 0
    low = jnp.where(odd, both[C1 : 2 * C1], both[:C1])
    high = jnp.where(odd, both[3 * C1 :], both[2 * C1 : 3 * C1])
    return jnp.where(upper, high, low).astype(bf16)


def scatter_four(values, row, first):
    place_four = (row >> 8) & 3
    zero = jnp.zeros_like(values)
    spread = jnp.concatenate(
        [jnp.where(place_four == w, values, zero) for w in range(4)], axis=0
    )
    return dot_nt(spread, one_hot(in_table(row, first), 256))


class Position:
    def __init__(self):
        self.dp, self.space = place()
        self.y, self.core = self.dp // 2, self.dp % 2
        self.z, self.x = self.space // 4, self.space % 4

    def brick(self, direction, sign):
        dy, dx = directions[direction]
        gy = (self.space // 8 + sign * dy + 4) % 4
        gx = (self.space % 8 + sign * dx + 8) % 8
        return (self.dp, gy * 8 + gx)

    def other_core(self):
        return (self.y * 2 + 1 - self.core, self.space)

    def at_y(self, y):
        return (y * 2 + self.core, self.space)

    def at_x(self, x):
        return (self.dp, self.z * 4 + x)

    def at_z(self, z):
        return (self.dp, z * 4 + self.x)

    def gray(self, v):
        return (v + v // 2) % 2

    def flip(self, v):
        return v + 1 - 2 * (v % 2)

    def halving(self, axis, step):
        v, at = (self.y, self.at_y) if axis == "y" else (self.x, self.at_x)
        first = 1 - self.core if step == 0 else self.core
        keep = first * self.gray(v) + (1 - first) * (v // 2)
        return keep, at(first * self.flip(v) + (1 - first) * (3 - v))

    def at_axis(self, axis, offset):
        if axis == "y":
            return self.at_y((self.y + offset) % 4)
        return self.at_x((self.x + offset) % 4)

    def in_row(self, offset):
        return ((self.dp + offset) % 8, self.space)

    def partners(self):
        return (
            [self.brick(d, 1) for d in range(8)]
            + [self.in_row(offset) for offset in range(1, 8)]
            + [self.at_axis("x", offset) for offset in range(1, 4)]
            + [self.at_z((self.z + offset) % 8) for offset in (1, 3, 4, 5, 7)]
        )


def add_into(target, index, source, start, count):
    def part(i, _):
        here = index + (pl.ds(start + i * 16, 16),)
        total = target[here].astype(f32) + source[pl.ds(i * 16, 16)].astype(f32)
        target[here] = total.astype(bf16)
        return 0

    lax.fori_loop(0, count // 16, part, 0)


def block_index(core, axes, piece, space):
    z, x = space // 4, space % 4
    first, second = (piece, x) if axes == "yx" else (x, piece)
    return ring_place[core][first] * 32 + second * 8 + z


class Reduction:
    def __init__(self, pos, axes, refs, send, recv):
        self.pos, self.axes = pos, axes
        self.buf, self.from_core, self.from_step, self.from_axis = refs[:4]
        self.parts, self.from_z, self.total, self.landed = refs[4:]
        self.send, self.recv = send, recv

    def copy(self, source, target, sem, device):
        return remote(source, target, self.send.at[sem], self.recv.at[sem], device)

    def core_copy(self):
        pos = self.pos
        return self.copy(self.buf.at[1 - pos.core], self.from_core, 0, pos.other_core())

    def base(self, half, steps):
        start, size = 0, 128
        for step in range(steps):
            size //= 2
            start = start + self.pos.halving(self.axes[half][0], step)[0] * size
        return start

    def step_copy(self, half, step):
        size = 64 >> step
        keep, partner = self.pos.halving(self.axes[half][0], step)
        start = self.base(half, step) + (1 - keep) * size
        return self.copy(
            self.buf.at[self.pos.core, half, pl.ds(start, size)],
            self.from_step.at[half, pl.ds(128 - 2 * size, size)],
            1 + half * 2 + step,
            partner,
        )

    def axis_block(self, half, offset):
        v = self.pos.x if self.axes[half] == "yx" else self.pos.y
        return self.base(half, 2) + (v + offset) % 4 * 8

    def axis_copy(self, half, offset):
        return self.copy(
            self.buf.at[self.pos.core, half, pl.ds(self.axis_block(half, offset), 8)],
            self.from_axis.at[half, offset - 1],
            4 + half * 3 + offset,
            self.pos.at_axis(self.axes[half][1], offset),
        )

    def z_copy(self, offset):
        z = (self.pos.z + offset) % 8
        return self.copy(
            self.parts.at[z], self.from_z.at[offset - 1], 10 + offset, self.pos.at_z(z)
        )

    def delivery(self, offset):
        return self.copy(
            self.total, self.landed.at[offset], 17 + offset, self.pos.in_row(offset)
        )

    def stage(self, number):
        pos = self.pos
        halves = range(len(self.axes))
        if number == 0:
            self.core_copy().start()
        elif number == 1:
            self.core_copy().wait()
            for half in halves:
                add_into(self.buf, (pos.core, half), self.from_core.at[half], 0, 128)
                self.step_copy(half, 0).start()
        elif number <= 3:
            size = 64 >> (number - 2)
            for half in halves:
                self.step_copy(half, number - 2).wait()
                add_into(
                    self.buf,
                    (pos.core, half),
                    self.from_step.at[half, pl.ds(128 - 2 * size, size)],
                    self.base(half, number - 1),
                    size,
                )
                if number == 2:
                    self.step_copy(half, 1).start()
                else:
                    for offset in range(1, 4):
                        self.axis_copy(half, offset).start()
        elif number == 4:
            for half in halves:
                for offset in range(1, 4):
                    self.axis_copy(half, offset).wait()
                own = self.buf[pos.core, half, pl.ds(self.axis_block(half, 0), 8)].astype(f32)
                for offset in range(3):
                    own = own + self.from_axis[half, offset].astype(f32)
                self.parts[:, half] = own.astype(bf16)
            for offset in range(1, 8):
                self.z_copy(offset).start()
        elif number == 5:
            for offset in range(1, 8):
                self.z_copy(offset).wait()
            total = self.parts[pos.z].astype(f32)
            for offset in range(7):
                total = total + self.from_z[offset].astype(f32)
            self.total[...] = total.astype(bf16)
            for offset in range(1, 8):
                self.delivery(offset).start()
        else:
            for offset in range(1, 8):
                self.delivery(offset).wait()
            self.landed[0] = self.total[...]

    def result(self, core, piece):
        return self.landed[(self.pos.dp - (piece * 2 + core) + 8) % 8]


def kernel(
    feature,
    w1_hbm,
    wd_hbm,
    w2_hbm,
    upstream,
    rule1,
    rule2,
    child,
    send1,
    send2,
    count1,
    count2,
    coarse_out,
    input_grad,
    wide_out,
    thin_out,
    w1,
    wd,
    w2,
    table1,
    halo1,
    pack1,
    picked1,
    act1,
    pickedd,
    actd,
    coarse,
    pack2,
    halo2,
    picked2,
    back2,
    ext_grad2,
    give2,
    take2,
    grad_level,
    back1,
    ext_grad1,
    give1,
    take1,
    strips,
    wide_buf,
    wide_core,
    wide_step,
    wide_axis,
    wide_parts,
    wide_z,
    wide_total,
    wide_land,
    thin_buf,
    thin_core,
    thin_step,
    thin_axis,
    thin_parts,
    thin_z,
    thin_total,
    thin_land,
    load_sem,
    halo_send,
    halo_recv,
    wide_send,
    wide_recv,
    thin_send,
    thin_recv,
):
    pos = Position()
    greet(pos.partners())
    wide_refs = (wide_buf, wide_core, wide_step, wide_axis, wide_parts, wide_z, wide_total, wide_land)
    thin_refs = (thin_buf, thin_core, thin_step, thin_axis, thin_parts, thin_z, thin_total, thin_land)
    wide = Reduction(pos, ("yx", "xy"), wide_refs, wide_send, wide_recv)
    thin = Reduction(pos, ("yx",), thin_refs, thin_send, thin_recv)
    loads = [
        pltpu.make_async_copy(source, target, load_sem.at[i])
        for i, (source, target) in enumerate([(w1_hbm, w1), (wd_hbm, wd), (w2_hbm, w2)])
    ]
    for load in loads:
        load.start()

    def live_rows(rows, counts, width):
        lane = lax.broadcasted_iota(i32, (1, width), 1)
        return jnp.concatenate(
            [jnp.where(lane < counts[d], rows[d : d + 1, :], -1) for d in range(8)], axis=1
        )

    def exchange(number, source, target, sign):
        return [
            remote(
                source(d),
                target(d),
                halo_send.at[number, d],
                halo_recv.at[number, d],
                pos.brick(d, sign),
            )
            for d in range(8)
        ]

    def folded(d):
        return (pl.ds(d // 2 * C1, C1), pl.ds(d % 2 * H1, H1))

    def tap_rows(k, channels):
        return pl.ds(pl.multiple_of(k * channels, channels), channels)

    def fold(target, values):
        for w in range(4):
            target[w * C1 : (w + 1) * C1, :] = values[:, w * 256 : (w + 1) * 256]

    def unfold(values):
        return jnp.concatenate([values[w * C1 : (w + 1) * C1] for w in range(4)], axis=1)

    live1 = live_rows(send1, count1, H1)
    fold(table1, feature[...])
    pack1[...] = gather_four(table1[...], live1, 0)
    await_greetings(pos.partners())
    copies = exchange(
        0, lambda d: pack1.at[:, pl.ds(d * H1, H1)], lambda d: halo1.at[folded(d)], 1
    )
    for copy in copies:
        copy.start()
    strips[...] = jnp.zeros_like(strips)
    picked2[TAPS * C2 :, :] = jnp.zeros((128, C2), bf16)

    def tap_one(k, _):
        picked1[tap_rows(k, C1), :] = gather_four(table1[...], rule1[k], 0)
        return 0

    lax.fori_loop(0, TAPS, tap_one, 0, unroll=9)
    for copy in copies:
        copy.wait()

    def tap_one_halo(k, _):
        here = (tap_rows(k, C1), slice(None))
        picked1[here] = picked1[here] + gather_four(halo1[...], rule1[k], V)
        return 0

    lax.fori_loop(0, TAPS, tap_one_halo, 0, unroll=9)
    loads[0].wait()
    act = dot(w1[...], picked1[...])
    act1[...] = act
    fold(table1, (feature[...].astype(f32) + silu(act)).astype(bf16))

    for m in range(8):
        pickedd[m * C1 : (m + 1) * C1, :] = gather_four(table1[...], child[m : m + 1, :], 0)
    loads[1].wait()
    act = dot(wd[...], pickedd[...])
    actd[...] = act
    coarse[...] = silu(act).astype(bf16)

    live2 = live_rows(send2, count2, H2)
    pack2[...] = dot(coarse[...], one_hot(live2, V2)).T.astype(bf16)
    copies = exchange(
        1, lambda d: pack2.at[pl.ds(d * H2, H2)], lambda d: halo2.at[pl.ds(d * H2, H2)], 1
    )
    for copy in copies:
        copy.start()

    def tap_two(k, _):
        picked2[tap_rows(k, C2), :] = dot(coarse[...], one_hot(rule2[k], V2)).astype(bf16)
        return 0

    lax.fori_loop(0, TAPS, tap_two, 0, unroll=9)
    for copy in copies:
        copy.wait()
    halo2[...] = halo2[...].astype(f32).T.astype(bf16)

    def tap_two_halo(k, _):
        here = (tap_rows(k, C2), slice(None))
        mine = dot(halo2[...], one_hot(rule2[k] - V2, V2)).astype(bf16)
        picked2[here] = picked2[here] + mine
        return 0

    lax.fori_loop(0, TAPS, tap_two_halo, 0, unroll=9)
    loads[2].wait()
    act = dot(w2[...], picked2[: TAPS * C2, :])
    coarse_out[...] = (coarse[...].astype(f32) + silu(act)).astype(bf16)
    grad_two = (upstream[...].astype(f32) * silu_grad(act)).astype(bf16)

    def spread_two(first):
        ext_grad2[...] = jnp.zeros_like(ext_grad2)

        def taps(t, _):
            total = ext_grad2[...]
            for j in range(9):
                k = t * 9 + j
                total += dot_nt(back2[tap_rows(k, C2), :], one_hot(rule2[k] - first, V2))
            ext_grad2[...] = total
            return 0

        lax.fori_loop(0, TAPS // 9, taps, 0)

    back2[...] = dot_tn(w2[...], grad_two).astype(bf16)
    spread_two(V2)
    give2[...] = ext_grad2[...].T.astype(bf16)
    copies = exchange(
        2, lambda d: give2.at[pl.ds(d * H2, H2)], lambda d: take2.at[pl.ds(d * H2, H2)], -1
    )
    for copy in copies:
        copy.start()
    for quarter in range(4):
        core, half = quarter // 2, quarter % 2
        upper = dot_nt(grad_two, picked2[quarter * WIDE : (quarter + 1) * WIDE, :])
        start = TAPS * V2 // 2 + quarter * WIDE
        lower = dot_nt(grad_two, picked2[start : start + WIDE, :])
        both = jnp.concatenate([upper.reshape(32, 8, WIDE), lower.reshape(32, 8, WIDE)], axis=1)
        both = both.astype(bf16)
        for piece in range(4):
            low = min(piece * WIDE_PIECE, WIDE - WIDE_PIECE)
            for space in range(32):
                block = block_index(core, wide.axes[half], piece, space)
                wide_buf[core, half, block] = both[space][:, low : low + WIDE_PIECE]
    wide.stage(0)
    spread_two(0)
    wide.stage(1)
    for copy in copies:
        copy.wait()
    returned = dot(one_hot(live2, V2), take2[...]).T
    grad_coarse = upstream[...].astype(f32) + ext_grad2[...] + returned
    grad_down = (grad_coarse * silu_grad(actd[...])).astype(bf16)

    backd = dot_tn(wd[...], grad_down).astype(bf16)
    total = jnp.zeros((4 * C1, 256), f32)
    for m in range(8):
        total += scatter_four(backd[m * C1 : (m + 1) * C1], child[m : m + 1, :], 0)
    grad_level[...] = total
    grad_one = (unfold(total) * silu_grad(act1[...])).astype(bf16)
    term_down = dot_nt(grad_down, pickedd[...]).reshape(32, 8, 768)
    term_one = dot_nt(grad_one, picked1[...]).astype(bf16)
    for q in range(5):
        width = min(640, TAPS * C1 - q * 640)
        strips[q * C1 : (q + 1) * C1, :width] = term_one[:, q * 640 : q * 640 + width]
    spot = lax.broadcasted_iota(i32, (1, 5 * C1), 1)
    strip, out_row = spot // C1, spot % C1
    spot = (out_row // 3) * 16 + (out_row % 3) * 5 + strip
    first = dot(one_hot(spot, 512), strips[...]).reshape(32, 16, 640)
    other = jnp.concatenate([term_down[:, :, :384], term_down[:, :, 384:]], axis=1)
    for tile in range(8):
        core, piece = tile // 4, tile % 4
        both = first if tile < 5 else other
        low = tile % 5 * THIN_PIECE
        both = both[:, :, low : low + THIN_PIECE].astype(bf16)
        for space in range(32):
            thin_buf[core, 0, block_index(core, thin.axes[0], piece, space)] = both[space]
    thin.stage(0)
    wide.stage(2)

    back1[...] = dot_tn(w1[...], grad_one).astype(bf16)

    def spread_one(first, beside):
        ext_grad1[...] = jnp.zeros_like(ext_grad1)

        def taps(t, _):
            for when, stages in beside.items():

                @pl.when(t == when)
                def _():
                    for reduction, number in stages:
                        reduction.stage(number)

            total = ext_grad1[...]
            for j in range(9):
                k = t * 9 + j
                total += scatter_four(back1[tap_rows(k, C1), :], rule1[k], first)
            ext_grad1[...] = total
            return 0

        lax.fori_loop(0, TAPS // 9, taps, 0)

    spread_one(V, {1: [(thin, 1)], 2: [(wide, 3)]})
    give1[...] = ext_grad1[...].astype(bf16)
    copies = exchange(
        3, lambda d: give1.at[folded(d)], lambda d: take1.at[:, pl.ds(d * H1, H1)], -1
    )
    for copy in copies:
        copy.start()
    thin.stage(2)
    spread_one(0, {1: [(wide, 4)], 2: [(thin, 3)]})
    thin.stage(4)
    wide.stage(5)
    for copy in copies:
        copy.wait()
    total = grad_level[...] + ext_grad1[...] + scatter_four(take1[...], live1, 0)
    input_grad[...] = unfold(total).astype(bf16)
    thin.stage(5)
    wide.stage(6)
    thin.stage(6)
    for core in range(2):
        for piece in range(4):
            thin_out[core, piece] = thin.result(core, piece)
            wide_out[core, piece] = wide.result(core, piece)


def finish(coarse_in, input_in, wide_in, thin_in, coarse_out, input_grad, gw1, gwd, gw2):
    coarse_out[...] = coarse_in[...]
    input_grad[...] = input_in[...]
    scale = 1.0 / 256
    for quarter in range(4):
        core, half = quarter // 2, quarter % 2
        piece = [wide_in[core, j, half] for j in range(4)]
        piece[3] = piece[3][:, 4 * WIDE_PIECE - WIDE :]
        piece = jnp.concatenate(piece, axis=1).astype(f32) * scale
        for side in range(2):
            start = quarter * WIDE
            width = min(WIDE, TAPS * V2 // 2 - start)
            here = side * TAPS * V2 // 2 + start
            gw2[:, here : here + width] = piece[side * 8 : side * 8 + 8, :width]
    pieces = [thin_in[q // 4, q % 4, 0].astype(f32) * scale for q in range(8)]
    thin_all = jnp.concatenate(pieces, axis=1)
    gwd[:, :384] = thin_all[:8, 640:]
    gwd[:, 384:] = thin_all[8:, 640:]
    for r in range(3):
        for q in range(5):
            width = min(640, TAPS * C1 - q * 640)
            row = r * 5 + q
            gw1[r : r + 1, q * 640 : q * 640 + width] = thin_all[row : row + 1, :width]


def reduction_scratch(halves, lanes):
    return [
        pltpu.VMEM((2, halves, 128, 16, lanes), bf16),
        pltpu.VMEM((halves, 128, 16, lanes), bf16),
        pltpu.VMEM((halves, 96, 16, lanes), bf16),
        pltpu.VMEM((halves, 3, 8, 16, lanes), bf16),
        pltpu.VMEM((8, halves, 16, lanes), bf16),
        pltpu.VMEM((7, halves, 16, lanes), bf16),
        pltpu.VMEM((halves, 16, lanes), bf16),
        pltpu.VMEM((8, halves, 16, lanes), bf16),
    ]


def run_kernels(*operands):
    vmem = pl.BlockSpec(memory_space=pltpu.VMEM)
    smem = pl.BlockSpec(memory_space=pltpu.SMEM)
    away = pl.BlockSpec(memory_space=pl.ANY)
    dma = pltpu.SemaphoreType.DMA
    results = pl.pallas_call(
        kernel,
        out_shape=(
            jax.ShapeDtypeStruct((C2, V2), bf16),
            jax.ShapeDtypeStruct((C1, V), bf16),
            jax.ShapeDtypeStruct((2, 4, 2, 16, WIDE_PIECE), bf16),
            jax.ShapeDtypeStruct((2, 4, 1, 16, THIN_PIECE), bf16),
        ),
        in_specs=[vmem] + [away] * 3 + [vmem] * 6 + [smem] * 2,
        out_specs=[vmem] * 4,
        scratch_shapes=[
            pltpu.VMEM((C1, TAPS * C1), bf16),
            pltpu.VMEM((C2, 8 * C1), bf16),
            pltpu.VMEM((C2, TAPS * C2), bf16),
            pltpu.VMEM((4 * C1, 256), bf16),
            pltpu.VMEM((4 * C1, 256), bf16),
            pltpu.VMEM((C1, V), bf16),
            pltpu.VMEM((TAPS * C1, V), bf16),
            pltpu.VMEM((C1, V), f32),
            pltpu.VMEM((8 * C1, V2), bf16),
            pltpu.VMEM((C2, V2), f32),
            pltpu.VMEM((C2, V2), bf16),
            pltpu.VMEM((V2, C2), bf16),
            pltpu.VMEM((V2, C2), bf16),
            pltpu.VMEM((TAPS * C2 + 128, V2), bf16),
            pltpu.VMEM((TAPS * C2, V2), bf16),
            pltpu.VMEM((C2, V2), f32),
            pltpu.VMEM((V2, C2), bf16),
            pltpu.VMEM((V2, C2), bf16),
            pltpu.VMEM((4 * C1, 256), f32),
            pltpu.VMEM((TAPS * C1, V), bf16),
            pltpu.VMEM((4 * C1, 256), f32),
            pltpu.VMEM((4 * C1, 256), bf16),
            pltpu.VMEM((C1, V), bf16),
            pltpu.VMEM((5 * C1, 640), bf16),
            *reduction_scratch(2, WIDE_PIECE),
            *reduction_scratch(1, THIN_PIECE),
            dma((3,)),
            dma((4, 8)),
            dma((4, 8)),
            dma((26,)),
            dma((26,)),
            dma((26,)),
            dma((26,)),
        ],
        compiler_params=pltpu.CompilerParams(
            collective_id=0, has_side_effects=True, vmem_limit_bytes=58 << 20
        ),
    )(*operands)
    return pl.pallas_call(
        finish,
        out_shape=(
            jax.ShapeDtypeStruct((C2, V2), bf16),
            jax.ShapeDtypeStruct((C1, V), bf16),
            jax.ShapeDtypeStruct((3, TAPS * C1), f32),
            jax.ShapeDtypeStruct((8, 8 * C1), f32),
            jax.ShapeDtypeStruct((8, TAPS * C2), f32),
        ),
        in_specs=[vmem] * 4,
        out_specs=[vmem] * 5,
    )(*results)


def body(
    features,
    weight_one,
    weight_down,
    weight_two,
    cotangent,
    rule_one,
    rule_two,
    children,
    send_one,
    count_one,
    send_two,
    count_two,
):
    coarse_out, input_grad, gw1, gwd, gw2 = run_kernels(
        features[0],
        weight_one,
        weight_down,
        weight_two,
        cotangent[0],
        rule_one.transpose(1, 0, 2),
        rule_two.transpose(1, 0, 2),
        children[0],
        send_one[0, 0],
        send_two[0, 0],
        count_one[0, 0],
        count_two[0, 0],
    )
    return coarse_out[None], input_grad[None], gw1, gwd, gw2


def solution(mesh):
    tile = P("dp", None, "space")
    brick = P("dp", "space", None, None)
    count = P("dp", "space", None)
    return jax.shard_map(
        body,
        mesh=mesh,
        in_specs=(tile, P(), P(), P(), tile, tile, tile, tile, brick, count, brick, count),
        out_specs=(tile, tile, P("space", None), P("space", None), P("space", None)),
        check_vma=False,
    )
```
